768 devices in a mesh: dp: 192 (over y, z, x_hi), node: 4 (over x_lo, core).
Axes of the slice: x: 4 (x_hi: 2, x_lo: 2; x = x_hi * 2 + x_lo), y: 8, z: 12, core: 2. Of those that a mesh axis runs over, the one named last changes fastest.
Arguments:
- gate_up: bfloat16 [196608, 240], P(('dp', 'node')), may hold values from -6 to 6
- out_grad: bfloat16 [196608, 8192], P(('dp', 'node')), may hold values from -6 to 6
- weight_codes: bfloat16 [120, 8192], P('node'), may hold values from -440 to 440
- weight_scales: bfloat16 [120, 64], P('node'), may hold values from 2.9921532e-05 to 0.00029945374
- shard_order: int32 [768], replicated, may hold values from 0 to 767, each once
Outputs:
- grad_gate_up: bfloat16 [196608, 240], P(('dp', 'node'))
- weight_grad: float32 [768, 1280], P(('dp', 'node'))
The draws below stay inside these ranges and needn't reach their ends.
Inputs may be any that keep to these rules, and one draw needn't show every extreme that they name: `shard_order`: a permutation: every span has exactly one owner.
All inputs are finite; a program needn't handle non-finite values.
Results may differ from the reference program's by a relative error of at most 0.014.
Values may be sent and summed in bfloat16 or wider, within the bound.
No kernel may reach another device: no remote copies, remote signals or barrier semaphores. Data moves between devices by JAX's collectives and lax.ppermute only.
A program may use at most 64 MiB of HBM per device.

```python
import math
import jax
import jax.numpy as jnp
from jax import lax

D = 8192
FW = 120
TOK_DEV = 256
QBLK = 128
TOKENS = 196608
N_DP = 192
N_NODE = 4
DEVICES = 768


def levels(key, extent, shards, least, top_value):
    loudness = 1.0
    for dim, parts in shards:
        heights = jax.random.uniform(jax.random.fold_in(jax.random.fold_in(key, 6), dim), (parts,), jnp.float32, least / len(shards), top_value / len(shards))
        loudness = loudness * jnp.repeat(jnp.exp(heights), extent[dim] // parts).reshape((-1,) + (1,) * (len(extent) - 1 - dim))
    return loudness


def scatter_about(rng, dims, scale, reach, pieces=(), kind=jnp.bfloat16):
    result = jax.random.normal(rng, dims, jnp.float32) * scale
    if len(pieces) > 0:
        result = levels(rng, dims, pieces, -0.22, 0.18) * result
    return jnp.clip(result, min=-reach, max=reach).astype(kind)


def setup_inputs(seed: int = 0) -> dict:
    splits = jax.random.split(jax.random.key(seed), 6)
    gate_up = scatter_about(splits[0], (TOKENS, 2 * FW), 1.0, 6.0, ((0, 768),))
    out_grad = scatter_about(splits[1], (TOKENS, D), 1.0, 6.0, ((0, 768),))
    weight_codes = scatter_about(splits[2], (FW, D), 100.0, 440.0, ((0, 4),))
    weight_scales = jnp.clip(jnp.exp(math.log(0.00029945374) - 2.3033816 * jax.random.uniform(splits[3], (FW, D // QBLK), jnp.float32) ** levels(splits[3], (FW, D // QBLK), ((0, 4),), -0.2, 0.2)), 2.9921531677246094e-05, 0.00029945374).astype(jnp.bfloat16)
    shard_order = jax.random.permutation(splits[4], DEVICES).astype(jnp.int32)
    return dict(gate_up=gate_up, out_grad=out_grad, weight_codes=weight_codes, weight_scales=weight_scales, shard_order=shard_order)


epsilon = 1e-6
code_limit = 448.0


def quantize(values):
    largest = jnp.max(jnp.abs(values), axis=-1)
    block_scale = ((largest + epsilon) / code_limit).astype(jnp.bfloat16)
    code_values = (values / block_scale.astype(jnp.float32)[..., None]).astype(jnp.bfloat16)
    return code_values, block_scale


def dequantize(code_values, block_scale):
    return code_values.astype(jnp.float32) * block_scale.astype(jnp.float32)[..., None]


def dequant_weight(weight_codes, weight_scales):
    rows_here = weight_codes.shape[0]
    blocked = weight_codes.reshape(rows_here, -1, QBLK)
    return dequantize(blocked, weight_scales).reshape(rows_here, -1).astype(jnp.bfloat16)


def local_terms(gate_up, out_grad, weight):
    half = gate_up.shape[1] // 2
    gate_pre = gate_up[:, :half].astype(jnp.float32)
    up_pre = gate_up[:, half:].astype(jnp.float32)
    sigmoid_gate = jax.nn.sigmoid(gate_pre)
    activated = gate_pre * sigmoid_gate
    hidden = (activated * up_pre).astype(jnp.bfloat16)
    hidden_grad = jnp.dot(out_grad, weight.T, preferred_element_type=jnp.float32)
    gate_grad = hidden_grad * up_pre * sigmoid_gate * (1.0 + gate_pre * (1.0 - sigmoid_gate))
    up_grad = hidden_grad * activated
    input_grad = jnp.concatenate([gate_grad, up_grad], axis=1).astype(jnp.bfloat16)
    partial_value = jnp.dot(hidden.T, out_grad, preferred_element_type=jnp.float32)
    return input_grad, partial_value


def reference(gate_up, out_grad, weight_codes, weight_scales, shard_order):
    weight = dequant_weight(weight_codes, weight_scales)

    def member_terms(member_gate_up, member_out_grad):
        input_grad, partial_value = local_terms(member_gate_up, member_out_grad, weight)
        spans = partial_value.reshape(DEVICES, -1, QBLK)[shard_order]
        code_values, block_scale = quantize(spans)
        return input_grad, dequantize(code_values, block_scale)

    def group_step(running, inputs):
        group_gate_up, group_out_grad = inputs
        input_grads, sent = jax.vmap(member_terms)(group_gate_up, group_out_grad)
        group_total = jnp.sum(sent, axis=0)
        code_values, block_scale = quantize(group_total)
        return running + dequantize(code_values, block_scale), input_grads

    running_start = jnp.zeros((DEVICES, FW * D // QBLK // DEVICES, QBLK), jnp.float32)
    inputs = (gate_up.reshape(N_DP, N_NODE, TOK_DEV, 2 * FW), out_grad.reshape(N_DP, N_NODE, TOK_DEV, D))
    final, input_grads = lax.scan(group_step, running_start, inputs)
    weight_grad = (final * (1.0 / DEVICES)).reshape(DEVICES, -1)
    return input_grads.reshape(TOKENS, 2 * FW), weight_grad
```

```python
import jax
import jax.numpy as jnp
from jax import lax
from jax.experimental import pallas as pl
from jax.experimental.pallas import tpu as pltpu
from jax.sharding import Mesh
from jax.sharding import PartitionSpec as P

D = 8192
FW = 120
TOK = 256
QBLK = 128
SPAN = 10
DEVICES = 768
NY, NZ = 8, 12
NX = 4
NYZ = NY * NZ
ROWS = DEVICES * SPAN
HALF = ROWS // 2
XROWS = HALF // NX
NODE_ROWS = 30
PAD_ROWS = 32
BLOCKS = D // QBLK
STEP_BLOCKS = 8
STEPS = BLOCKS // STEP_BLOCKS
ALL = ("y", "z", "xh", "xl", "core")
X = ("xh", "xl")
YZ = ("y", "z")


def dequant_kernel(codes_ref, scales_ref, out_ref):
    scales = scales_ref[...].astype(jnp.float32)
    fill = jnp.zeros((PAD_ROWS - NODE_ROWS, QBLK), jnp.float32)
    for block in range(BLOCKS):
        columns = slice(block * QBLK, (block + 1) * QBLK)
        value = codes_ref[:, columns].astype(jnp.float32) * scales[:, block : block + 1]
        out_ref[:, columns] = jnp.concatenate([value, fill], axis=0).astype(jnp.bfloat16)


def dequant(codes, scales):
    return pl.pallas_call(
        dequant_kernel,
        out_shape=jax.ShapeDtypeStruct((PAD_ROWS, D), jnp.bfloat16),
        cost_estimate=pl.CostEstimate(flops=PAD_ROWS * D, bytes_accessed=4 * PAD_ROWS * D, transcendentals=0),
    )(codes, scales)


def partial_kernel(order_ref, core_ref, gate_up_ref, out_grad_ref, keep_ref, send_ref, hidden, blocks, staged):
    step = pl.program_id(0)

    @pl.when(step == 0)
    def _():
        both = gate_up_ref[...].astype(jnp.float32)
        gate, up = both[:FW], both[FW:]
        hidden[...] = (gate * jax.nn.sigmoid(gate) * up).astype(jnp.bfloat16)

    product = jnp.dot(hidden[...], out_grad_ref[...], preferred_element_type=jnp.float32)
    for block in range(STEP_BLOCKS):
        blocks[pl.ds(step * STEP_BLOCKS + block, FW, stride=BLOCKS), :] = product[:, block * QBLK : (block + 1) * QBLK]

    @pl.when(step == STEPS - 1)
    def _():
        core = core_ref[0]

        def gather(yz, carry):
            for low in range(8):
                x, owner_core = low // 2, low % 2
                span = order_ref[yz * 8 + low]
                value = blocks[pl.ds(span * SPAN, SPAN), :]
                place = (x * NYZ + yz) * SPAN

                @pl.when(core == owner_core)
                def _():
                    keep_ref[pl.ds(place, SPAN), :] = value

                @pl.when(core != owner_core)
                def _():
                    staged[pl.ds(place, SPAN), :] = value

            return carry

        lax.fori_loop(0, NYZ, gather, 0)
        send_ref[...] = staged[...].astype(jnp.bfloat16)


def partial_spans(order, core, gate_up_t, out_grad):
    width = STEP_BLOCKS * QBLK
    whole = lambda i, *_: (0, 0)
    return pl.pallas_call(
        partial_kernel,
        grid_spec=pltpu.PrefetchScalarGridSpec(
            num_scalar_prefetch=2,
            grid=(STEPS,),
            in_specs=[
                pl.BlockSpec((2 * FW, TOK), whole),
                pl.BlockSpec((TOK, width), lambda i, *_: (0, i)),
            ],
            out_specs=[pl.BlockSpec((HALF, QBLK), whole), pl.BlockSpec((HALF, QBLK), whole)],
            scratch_shapes=[
                pltpu.VMEM((FW, TOK), jnp.bfloat16),
                pltpu.VMEM((ROWS, QBLK), jnp.float32),
                pltpu.VMEM((HALF, QBLK), jnp.float32),
            ],
        ),
        out_shape=[
            jax.ShapeDtypeStruct((HALF, QBLK), jnp.float32),
            jax.ShapeDtypeStruct((HALF, QBLK), jnp.bfloat16),
        ],
        compiler_params=pltpu.CompilerParams(vmem_limit_bytes=24 * 2**20),
        cost_estimate=pl.CostEstimate(flops=2 * FW * TOK * D, bytes_accessed=2 * TOK * D + 6 * HALF * QBLK, transcendentals=FW * TOK),
    )(order, core, gate_up_t, out_grad)


def grads_kernel(gate_up_ref, weight_ref, out_grad_ref, out_ref, total):
    step = pl.program_id(0)
    product = lax.dot_general(
        weight_ref[...], out_grad_ref[...], (((1,), (1,)), ((), ())), preferred_element_type=jnp.float32
    )

    @pl.when(step == 0)
    def _():
        total[...] = product

    @pl.when(step > 0)
    def _():
        total[...] += product

    @pl.when(step == STEPS - 1)
    def _():
        hidden_grad = jnp.concatenate(
            [total[i * PAD_ROWS : i * PAD_ROWS + NODE_ROWS, :] for i in range(4)], axis=0
        )
        both = gate_up_ref[...].astype(jnp.float32)
        gate, up = both[:FW], both[FW:]
        sig = jax.nn.sigmoid(gate)
        gate_grad = hidden_grad * up * sig * (1.0 + gate * (1.0 - sig))
        up_grad = hidden_grad * (gate * sig)
        out_ref[...] = jnp.concatenate([gate_grad, up_grad], axis=0).astype(jnp.bfloat16)


def input_grads(gate_up_t, weight, out_grad):
    width = STEP_BLOCKS * QBLK
    whole = lambda i: (0, 0)
    return pl.pallas_call(
        grads_kernel,
        grid=(STEPS,),
        in_specs=[
            pl.BlockSpec((2 * FW, TOK), whole),
            pl.BlockSpec((4 * PAD_ROWS, width), lambda i: (0, i)),
            pl.BlockSpec((TOK, width), lambda i: (0, i)),
        ],
        out_specs=pl.BlockSpec((2 * FW, TOK), whole),
        out_shape=jax.ShapeDtypeStruct((2 * FW, TOK), jnp.bfloat16),
        scratch_shapes=[pltpu.VMEM((4 * PAD_ROWS, TOK), jnp.float32)],
        compiler_params=pltpu.CompilerParams(vmem_limit_bytes=12 * 2**20),
        cost_estimate=pl.CostEstimate(flops=2 * FW * TOK * D, bytes_accessed=2 * TOK * D + 2 * 128 * D, transcendentals=FW * TOK),
    )(gate_up_t, weight, out_grad)


def pair_sum_kernel(keep_ref, got_ref, out_ref):
    out_ref[...] = (keep_ref[...] + got_ref[...].astype(jnp.float32)).astype(jnp.bfloat16)


def pair_sum(keep, got):
    steps = 4
    spec = pl.BlockSpec((HALF // steps, QBLK), lambda i: (i, 0))
    return pl.pallas_call(
        pair_sum_kernel,
        grid=(steps,),
        in_specs=[spec, spec],
        out_specs=spec,
        out_shape=jax.ShapeDtypeStruct((HALF, QBLK), jnp.bfloat16),
    )(keep, got)


def x_sum_kernel(got_ref, out_ref):
    total = got_ref[:XROWS, :].astype(jnp.float32)
    for i in range(1, NX):
        total += got_ref[i * XROWS : (i + 1) * XROWS, :].astype(jnp.float32)
    out_ref[...] = total.astype(jnp.bfloat16)


def x_sum(got):
    return pl.pallas_call(
        x_sum_kernel,
        out_shape=jax.ShapeDtypeStruct((XROWS, QBLK), jnp.bfloat16),
    )(got)


def last_sum_kernel(got_ref, out_ref, total):
    rows = 8 * SPAN
    eight = got_ref[:rows, :].astype(jnp.float32)
    for i in range(1, XROWS // rows):
        eight += got_ref[i * rows : (i + 1) * rows, :].astype(jnp.float32)
    total[...] = eight
    span = total[:SPAN, :]
    for i in range(1, 8):
        span += total[i * SPAN : (i + 1) * SPAN, :]
    span = span * (1.0 / DEVICES)
    for i in range(SPAN):
        out_ref[:, i * QBLK : (i + 1) * QBLK] = span[i : i + 1, :]


def last_sum(got):
    return pl.pallas_call(
        last_sum_kernel,
        out_shape=jax.ShapeDtypeStruct((1, SPAN * QBLK), jnp.float32),
        scratch_shapes=[pltpu.VMEM((8 * SPAN, QBLK), jnp.float32)],
    )(got)


def per_device(gate_up, out_grad, weight_codes, weight_scales, shard_order):
    gate_up_t = gate_up.T
    core = lax.axis_index("core").astype(jnp.int32).reshape(1)
    weight = lax.all_gather(dequant(weight_codes, weight_scales), ("xl", "core"), axis=0, tiled=True)
    keep, send = partial_spans(shard_order, core, gate_up_t, out_grad)
    got = lax.ppermute(send, "core", [(0, 1), (1, 0)])
    pair = pair_sum(keep, got)
    got = lax.all_to_all(pair, X, split_axis=0, concat_axis=0, tiled=True)
    line = x_sum(got).reshape(XROWS // 2, 2, QBLK)
    got = lax.all_to_all(line, YZ, split_axis=0, concat_axis=0, tiled=True)
    weight_grad = last_sum(got.reshape(XROWS, QBLK))
    grad_gate_up = input_grads(gate_up_t, weight, out_grad).T
    return (grad_gate_up, weight_grad)


def solution(mesh):
    fine = Mesh(mesh.devices.reshape(NY, NZ, 2, 2, 2), ALL)
    return jax.shard_map(
        per_device,
        mesh=fine,
        in_specs=(P(ALL, None), P(ALL, None), P(("xl", "core"), None), P(("xl", "core"), None), P()),
        out_specs=(P(ALL, None), P(ALL, None)),
        check_vma=False,
    )
```

```python
import jax
import jax.numpy as jnp
from jax import lax
from jax.experimental import pallas as pl
from jax.experimental.pallas import tpu as pltpu
from jax.sharding import Mesh
from jax.sharding import PartitionSpec as P

D = 8192
FW = 120
TOK = 256
QBLK = 128
SPAN = 10
DEVICES = 768
NY, NZ = 8, 12
NX = 4
NYZ = NY * NZ
ROWS = DEVICES * SPAN
HALF = ROWS // 2
XROWS = HALF // NX
NODE_ROWS = 30
PAD_ROWS = 32
BLOCKS = D // QBLK
STEP_BLOCKS = 8
STEPS = BLOCKS // STEP_BLOCKS
WIDTH = STEP_BLOCKS * QBLK
SWAP = [(0, 1), (1, 0)]
ALL = ("y", "z", "xh", "xl", "core")
X = ("xh", "xl")
YZ = ("y", "z")


def partial_kernel(
    order_ref, core_ref, gate_up_ref, out_grad_ref, codes_ref, scales_ref, keep_ref, send_ref, weight_ref, hidden, blocks, staged
):
    step = pl.program_id(0)

    @pl.when(step == 0)
    def _():
        both = gate_up_ref[...].astype(jnp.float32)
        gate, up = both[:FW], both[FW:]
        hidden[...] = (gate * jax.nn.sigmoid(gate) * up).astype(jnp.bfloat16)

    product = jnp.dot(hidden[...], out_grad_ref[...], preferred_element_type=jnp.float32)
    for block in range(STEP_BLOCKS):
        blocks[pl.ds(step * STEP_BLOCKS + block, FW, stride=BLOCKS), :] = product[:, block * QBLK : (block + 1) * QBLK]

    block_of = lax.broadcasted_iota(jnp.int32, (BLOCKS, WIDTH), 1) // QBLK + step * STEP_BLOCKS
    one_hot = (lax.broadcasted_iota(jnp.int32, (BLOCKS, WIDTH), 0) == block_of).astype(jnp.float32).astype(jnp.bfloat16)
    scales = jnp.dot(scales_ref[...], one_hot, preferred_element_type=jnp.float32)
    weight = codes_ref[...].astype(jnp.float32) * scales
    fill = jnp.zeros((PAD_ROWS - NODE_ROWS, WIDTH), jnp.float32)
    weight_ref[...] = jnp.concatenate([weight, fill], axis=0).astype(jnp.bfloat16)

    @pl.when(step == STEPS - 1)
    def _():
        core = core_ref[0]
        first = (core * HALF, (1 - core) * HALF)

        def gather(yz, carry):
            for low in range(8):
                span = order_ref[yz * 8 + low]
                place = first[low % 2] + ((low // 2) * NYZ + yz) * SPAN
                staged[pl.ds(place, SPAN), :] = blocks[pl.ds(span * SPAN, SPAN), :]
            return carry

        lax.fori_loop(0, NYZ, gather, 0)
        keep_ref[...] = staged[:HALF, :].astype(jnp.bfloat16)
        send_ref[...] = staged[HALF:, :].astype(jnp.bfloat16)


def partial_spans(order, core, gate_up_t, out_grad, codes, scales):
    whole = lambda i, *_: (0, 0)
    columns = lambda i, *_: (0, i)
    return pl.pallas_call(
        partial_kernel,
        grid_spec=pltpu.PrefetchScalarGridSpec(
            num_scalar_prefetch=2,
            grid=(STEPS,),
            in_specs=[
                pl.BlockSpec((2 * FW, TOK), whole),
                pl.BlockSpec((TOK, WIDTH), columns),
                pl.BlockSpec((NODE_ROWS, WIDTH), columns),
                pl.BlockSpec((NODE_ROWS, BLOCKS), whole),
            ],
            out_specs=[
                pl.BlockSpec((HALF, QBLK), whole),
                pl.BlockSpec((HALF, QBLK), whole),
                pl.BlockSpec((PAD_ROWS, WIDTH), columns),
            ],
            scratch_shapes=[
                pltpu.VMEM((FW, TOK), jnp.bfloat16),
                pltpu.VMEM((ROWS, QBLK), jnp.float32),
                pltpu.VMEM((ROWS, QBLK), jnp.float32),
            ],
        ),
        out_shape=[
            jax.ShapeDtypeStruct((HALF, QBLK), jnp.bfloat16),
            jax.ShapeDtypeStruct((HALF, QBLK), jnp.bfloat16),
            jax.ShapeDtypeStruct((PAD_ROWS, D), jnp.bfloat16),
        ],
        compiler_params=pltpu.CompilerParams(vmem_limit_bytes=56 * 2**20),
        cost_estimate=pl.CostEstimate(flops=2 * FW * TOK * D, bytes_accessed=2 * TOK * D + 4 * HALF * QBLK, transcendentals=FW * TOK),
    )(order, core, gate_up_t, out_grad, codes, scales)


def grads_kernel(place_ref, gate_up_ref, own_ref, core_ref, x_ref, both_ref, out_grad_ref, out_ref, weight, total):
    step = pl.program_id(0)
    for i, part in enumerate((own_ref, core_ref, x_ref, both_ref)):
        row = pl.multiple_of(jnp.bitwise_xor(place_ref[0], i) * PAD_ROWS, PAD_ROWS)
        weight[pl.ds(row, PAD_ROWS), :] = part[...]
    product = lax.dot_general(
        weight[...], out_grad_ref[...], (((1,), (1,)), ((), ())), preferred_element_type=jnp.float32
    )

    @pl.when(step == 0)
    def _():
        total[...] = product

    @pl.when(step > 0)
    def _():
        total[...] += product

    @pl.when(step == STEPS - 1)
    def _():
        hidden_grad = jnp.concatenate(
            [total[i * PAD_ROWS : i * PAD_ROWS + NODE_ROWS, :] for i in range(4)], axis=0
        )
        both = gate_up_ref[...].astype(jnp.float32)
        gate, up = both[:FW], both[FW:]
        sig = jax.nn.sigmoid(gate)
        gate_grad = hidden_grad * up * sig * (1.0 + gate * (1.0 - sig))
        up_grad = hidden_grad * (gate * sig)
        out_ref[...] = jnp.concatenate([gate_grad, up_grad], axis=0).astype(jnp.bfloat16)


def input_grads(place, gate_up_t, parts, out_grad):
    whole = lambda i, *_: (0, 0)
    columns = lambda i, *_: (0, i)
    return pl.pallas_call(
        grads_kernel,
        grid_spec=pltpu.PrefetchScalarGridSpec(
            num_scalar_prefetch=1,
            grid=(STEPS,),
            in_specs=[pl.BlockSpec((2 * FW, TOK), whole)]
            + [pl.BlockSpec((PAD_ROWS, WIDTH), columns)] * 4
            + [pl.BlockSpec((TOK, WIDTH), columns)],
            out_specs=pl.BlockSpec((2 * FW, TOK), whole),
            scratch_shapes=[
                pltpu.VMEM((4 * PAD_ROWS, WIDTH), jnp.bfloat16),
                pltpu.VMEM((4 * PAD_ROWS, TOK), jnp.float32),
            ],
        ),
        out_shape=jax.ShapeDtypeStruct((2 * FW, TOK), jnp.bfloat16),
        compiler_params=pltpu.CompilerParams(vmem_limit_bytes=56 * 2**20),
        cost_estimate=pl.CostEstimate(flops=2 * FW * TOK * D, bytes_accessed=2 * TOK * D + 2 * 128 * D, transcendentals=FW * TOK),
    )(place, gate_up_t, *parts, out_grad)


def last_sum_kernel(got_ref, out_ref, total):
    rows = 8 * SPAN
    eight = got_ref[:rows, :].astype(jnp.float32)
    for i in range(1, XROWS // rows):
        eight += got_ref[i * rows : (i + 1) * rows, :].astype(jnp.float32)
    total[...] = eight
    span = total[:SPAN, :]
    for i in range(1, 8):
        span += total[i * SPAN : (i + 1) * SPAN, :]
    span = span * (1.0 / DEVICES)
    for i in range(SPAN):
        out_ref[:, i * QBLK : (i + 1) * QBLK] = span[i : i + 1, :]


def last_sum(got):
    return pl.pallas_call(
        last_sum_kernel,
        out_shape=jax.ShapeDtypeStruct((1, SPAN * QBLK), jnp.float32),
        scratch_shapes=[pltpu.VMEM((8 * SPAN, QBLK), jnp.float32)],
    )(got)


def per_device(gate_up, out_grad, weight_codes, weight_scales, shard_order):
    gate_up_t = gate_up.T
    core = lax.axis_index("core").astype(jnp.int32).reshape(1)
    place = lax.axis_index(("xl", "core")).astype(jnp.int32).reshape(1)
    keep, send, weight = partial_spans(shard_order, core, gate_up_t, out_grad, weight_codes, weight_scales)
    got = lax.ppermute(send, "core", SWAP)
    pair = (keep.astype(jnp.float32) + got.astype(jnp.float32)).astype(jnp.bfloat16)
    got = lax.all_to_all(pair, X, split_axis=0, concat_axis=0, tiled=True)
    parts = [got[i * XROWS : (i + 1) * XROWS].astype(jnp.float32) for i in range(NX)]
    line = (parts[0] + parts[1] + parts[2] + parts[3]).astype(jnp.bfloat16)
    line, weight = lax.optimization_barrier((line, weight))
    weight_x = lax.ppermute(weight, "xl", SWAP)
    weight_core = lax.ppermute(weight, "core", SWAP)
    weight_both = lax.ppermute(weight_x, "core", SWAP)
    got = lax.all_to_all(line.reshape(XROWS // 2, 2, QBLK), YZ, split_axis=0, concat_axis=0, tiled=True)
    grad_gate_up = input_grads(place, gate_up_t, (weight, weight_core, weight_x, weight_both), out_grad).T
    weight_grad = last_sum(got.reshape(XROWS, QBLK))
    return (grad_gate_up, weight_grad)


def solution(mesh):
    fine = Mesh(mesh.devices.reshape(NY, NZ, 2, 2, 2), ALL)
    return jax.shard_map(
        per_device,
        mesh=fine,
        in_specs=(P(ALL, None), P(ALL, None), P(("xl", "core"), None), P(("xl", "core"), None), P()),
        out_specs=(P(ALL, None), P(ALL, None)),
        check_vma=False,
    )
```

```python
import jax
import jax.numpy as jnp
from jax import lax
from jax.experimental import pallas as pl
from jax.experimental.pallas import tpu as pltpu
from jax.sharding import Mesh
from jax.sharding import PartitionSpec as P

D = 8192
FW = 120
TOK = 256
QBLK = 128
SPAN = 10
DEVICES = 768
NY, NZ = 8, 12
NX = 4
ROWS = DEVICES * SPAN
HALF = ROWS // 2
NODE_ROWS = 30
PAD_ROWS = 32
BLOCKS = D // QBLK
STEP_BLOCKS = 16
STEPS = BLOCKS // STEP_BLOCKS
WIDTH = STEP_BLOCKS * QBLK
SWAP = [(0, 1), (1, 0)]
ALL = ("y", "z", "xh", "xl", "core")
PLANE = ("y", "xh", "xl")


def read_columns(source, target, sems, chunk):
    columns = pl.ds(chunk * WIDTH, WIDTH)
    return pltpu.make_async_copy(source.at[:, columns], target.at[:, columns], sems.at[chunk])


def partial_kernel(
    core_ref, order_hbm, gate_up_hbm, out_grad_hbm, codes_hbm, scales_hbm, keep_ref, send_ref, weight_ref,
    order, gate_up, codes, scales, out_grad, blocks, staged, sems, small_sems,
):
    small = [
        pltpu.make_async_copy(source, target, small_sems.at[i])
        for i, (source, target) in enumerate(
            ((gate_up_hbm, gate_up), (scales_hbm, scales), (codes_hbm, codes), (order_hbm, order))
        )
    ]
    small[0].start()
    for chunk in range(STEPS):
        read_columns(out_grad_hbm, out_grad, sems, chunk).start()
    for read in small[1:]:
        read.start()
    small[0].wait()
    both = gate_up[...].astype(jnp.float32)
    gate, up = both[:FW], both[FW:]
    hidden = (gate * jax.nn.sigmoid(gate) * up).astype(jnp.bfloat16)
    for chunk in range(STEPS):
        columns = slice(chunk * WIDTH, (chunk + 1) * WIDTH)
        read_columns(out_grad_hbm, out_grad, sems, chunk).wait()
        product = jnp.dot(hidden, out_grad[:, columns], preferred_element_type=jnp.float32)
        for block in range(STEP_BLOCKS):
            blocks[pl.ds(chunk * STEP_BLOCKS + block, FW, stride=BLOCKS), :] = product[:, block * QBLK : (block + 1) * QBLK]
    for read in small[1:]:
        read.wait()
    fill = jnp.zeros((PAD_ROWS - NODE_ROWS, WIDTH), jnp.float32)
    for chunk in range(STEPS):
        columns = slice(chunk * WIDTH, (chunk + 1) * WIDTH)
        block_of = lax.broadcasted_iota(jnp.int32, (BLOCKS, WIDTH), 1) // QBLK + chunk * STEP_BLOCKS
        one_hot = (lax.broadcasted_iota(jnp.int32, (BLOCKS, WIDTH), 0) == block_of).astype(jnp.float32)
        wide = jnp.dot(scales[...], one_hot.astype(jnp.bfloat16), preferred_element_type=jnp.float32)
        weight = codes[:, columns].astype(jnp.float32) * wide
        weight_ref[:, columns] = jnp.concatenate([weight, fill], axis=0).astype(jnp.bfloat16)

    core = core_ref[0]
    first = (core * HALF, (1 - core) * HALF)

    def gather(y, carry):
        for z in range(NZ):
            for low in range(8):
                span = order[y * (8 * NZ) + z * 8 + low]
                place = first[low % 2] + y * (NX * NZ * SPAN) + ((low // 2) * NZ + z) * SPAN
                staged[pl.ds(place, SPAN), :] = blocks[pl.ds(span * SPAN, SPAN), :]
        return carry

    lax.fori_loop(0, NY, gather, 0)
    keep_ref[...] = staged[:HALF, :].astype(jnp.bfloat16)
    send_ref[...] = staged[HALF:, :].astype(jnp.bfloat16)


def partial_spans(order, core, gate_up_t, out_grad, codes, scales):
    hbm = pl.BlockSpec(memory_space=pltpu.HBM)
    vmem = pl.BlockSpec(memory_space=pltpu.VMEM)
    return pl.pallas_call(
        partial_kernel,
        in_specs=[pl.BlockSpec(memory_space=pltpu.SMEM)] + [hbm] * 5,
        out_specs=[vmem, vmem, vmem],
        scratch_shapes=[
            pltpu.SMEM((DEVICES,), jnp.int32),
            pltpu.VMEM((2 * FW, TOK), jnp.bfloat16),
            pltpu.VMEM((NODE_ROWS, D), jnp.bfloat16),
            pltpu.VMEM((NODE_ROWS, BLOCKS), jnp.bfloat16),
            pltpu.VMEM((TOK, D), jnp.bfloat16),
            pltpu.VMEM((ROWS, QBLK), jnp.float32),
            pltpu.VMEM((ROWS, QBLK), jnp.float32),
            pltpu.SemaphoreType.DMA((STEPS,)),
            pltpu.SemaphoreType.DMA((4,)),
        ],
        out_shape=[
            jax.ShapeDtypeStruct((HALF, QBLK), jnp.bfloat16),
            jax.ShapeDtypeStruct((HALF, QBLK), jnp.bfloat16),
            jax.ShapeDtypeStruct((PAD_ROWS, D), jnp.bfloat16),
        ],
        compiler_params=pltpu.CompilerParams(vmem_limit_bytes=56 * 2**20),
        cost_estimate=pl.CostEstimate(flops=2 * FW * TOK * D, bytes_accessed=2 * TOK * D + 4 * HALF * QBLK, transcendentals=FW * TOK),
    )(core, order, gate_up_t, out_grad, codes, scales)


def grads_kernel(place_ref, gate_up_ref, own_hbm, core_hbm, x_hbm, both_hbm, out_grad_hbm, out_ref, weight, out_grad, weight_sems, sems):
    reads = []
    for i, part in enumerate((own_hbm, core_hbm, x_hbm, both_hbm)):
        row = pl.multiple_of(jnp.bitwise_xor(place_ref[0], i) * PAD_ROWS, PAD_ROWS)
        reads.append(pltpu.make_async_copy(part, weight.at[pl.ds(row, PAD_ROWS), :], weight_sems.at[i]))
        reads[-1].start()
    for chunk in range(STEPS):
        read_columns(out_grad_hbm, out_grad, sems, chunk).start()
    both = gate_up_ref[...].astype(jnp.float32)
    gate, up = both[:FW], both[FW:]
    sig = jax.nn.sigmoid(gate)
    for read in reads:
        read.wait()
    total = jnp.zeros((TOK, 4 * PAD_ROWS), jnp.float32)
    for chunk in range(STEPS):
        columns = slice(chunk * WIDTH, (chunk + 1) * WIDTH)
        read_columns(out_grad_hbm, out_grad, sems, chunk).wait()
        total += lax.dot_general(
            out_grad[:, columns], weight[:, columns], (((1,), (1,)), ((), ())), preferred_element_type=jnp.float32
        )
    total = total.T
    hidden_grad = jnp.concatenate([total[i * PAD_ROWS : i * PAD_ROWS + NODE_ROWS, :] for i in range(4)], axis=0)
    gate_grad = hidden_grad * up * sig * (1.0 + gate * (1.0 - sig))
    up_grad = hidden_grad * (gate * sig)
    out_ref[...] = jnp.concatenate([gate_grad, up_grad], axis=0).astype(jnp.bfloat16)


def input_grads(place, gate_up_t, parts, out_grad):
    smem = pl.BlockSpec(memory_space=pltpu.SMEM)
    vmem = pl.BlockSpec(memory_space=pltpu.VMEM)
    anywhere = pl.BlockSpec(memory_space=pl.ANY)
    return pl.pallas_call(
        grads_kernel,
        in_specs=[smem, vmem] + [anywhere] * 4 + [pl.BlockSpec(memory_space=pltpu.HBM)],
        out_specs=vmem,
        scratch_shapes=[
            pltpu.VMEM((4 * PAD_ROWS, D), jnp.bfloat16),
            pltpu.VMEM((TOK, D), jnp.bfloat16),
            pltpu.SemaphoreType.DMA((4,)),
            pltpu.SemaphoreType.DMA((STEPS,)),
        ],
        out_shape=jax.ShapeDtypeStruct((2 * FW, TOK), jnp.bfloat16),
        compiler_params=pltpu.CompilerParams(vmem_limit_bytes=56 * 2**20),
        cost_estimate=pl.CostEstimate(flops=2 * FW * TOK * D, bytes_accessed=2 * TOK * D + 2 * 128 * D, transcendentals=FW * TOK),
    )(place, gate_up_t, *parts, out_grad)


def plane_sum_kernel(got_ref, out_ref):
    rows = 2 * NZ * SPAN
    total = got_ref[:rows, :].astype(jnp.float32)
    for i in range(1, HALF // rows):
        total += got_ref[i * rows : (i + 1) * rows, :].astype(jnp.float32)
    out_ref[...] = (total[: rows // 2] + total[rows // 2 :]).astype(jnp.bfloat16)


def plane_sum(got):
    return pl.pallas_call(
        plane_sum_kernel,
        in_specs=[pl.BlockSpec(memory_space=pltpu.VMEM)],
        out_specs=pl.BlockSpec(memory_space=pltpu.VMEM),
        out_shape=jax.ShapeDtypeStruct((NZ * SPAN, QBLK), jnp.bfloat16),
        compiler_params=pltpu.CompilerParams(vmem_limit_bytes=4 * 2**20),
    )(got)


def last_sum_kernel(got_ref, out_ref, spans):
    spans[...] = got_ref[...].astype(jnp.float32)
    span = spans[:SPAN, :]
    for i in range(1, NZ):
        span += spans[i * SPAN : (i + 1) * SPAN, :]
    span = span * (1.0 / DEVICES)
    for i in range(SPAN):
        out_ref[:, i * QBLK : (i + 1) * QBLK] = span[i : i + 1, :]


def last_sum(got):
    return pl.pallas_call(
        last_sum_kernel,
        in_specs=[pl.BlockSpec(memory_space=pltpu.VMEM)],
        out_specs=pl.BlockSpec(memory_space=pltpu.VMEM),
        out_shape=jax.ShapeDtypeStruct((1, SPAN * QBLK), jnp.float32),
        scratch_shapes=[pltpu.VMEM((NZ * SPAN, QBLK), jnp.float32)],
        compiler_params=pltpu.CompilerParams(vmem_limit_bytes=2 * 2**20),
    )(got)


def per_device(gate_up, out_grad, weight_codes, weight_scales, shard_order):
    gate_up_t = gate_up.T
    core = lax.axis_index("core").astype(jnp.int32).reshape(1)
    place = lax.axis_index(("xl", "core")).astype(jnp.int32).reshape(1)
    keep, send, weight = partial_spans(shard_order, core, gate_up_t, out_grad, weight_codes, weight_scales)
    got = lax.ppermute(send, "core", SWAP)
    weight_x = lax.ppermute(weight, "xl", SWAP)
    pair = (keep.astype(jnp.float32) + got.astype(jnp.float32)).astype(jnp.bfloat16)
    got = lax.all_to_all(pair, PLANE, split_axis=0, concat_axis=0, tiled=True)
    weight_x, weight = lax.optimization_barrier((weight_x, weight))
    weight_core = lax.ppermute(weight, "core", SWAP)
    weight_both = lax.ppermute(weight_x, "core", SWAP)
    grads = input_grads(place, gate_up_t, (weight, weight_core, weight_x, weight_both), out_grad)
    got, grads = lax.optimization_barrier((got, grads))
    line = plane_sum(got).reshape(NZ * SPAN // 2, 2, QBLK)
    got = lax.all_to_all(line, "z", split_axis=0, concat_axis=0, tiled=True)
    weight_grad = last_sum(got.reshape(NZ * SPAN, QBLK))
    return (grads.T, weight_grad)


def solution(mesh):
    fine = Mesh(mesh.devices.reshape(NY, NZ, 2, 2, 2), ALL)
    return jax.shard_map(
        per_device,
        mesh=fine,
        in_specs=(P(ALL, None), P(ALL, None), P(("xl", "core"), None), P(("xl", "core"), None), P()),
        out_specs=(P(ALL, None), P(ALL, None)),
        check_vma=False,
    )
```

```python
import jax
import jax.numpy as jnp
from jax import lax
from jax.experimental import pallas as pl
from jax.experimental.pallas import tpu as pltpu
from jax.sharding import Mesh
from jax.sharding import PartitionSpec as P

D = 8192
FW = 120
TOK = 256
QBLK = 128
SPAN = 10
DEVICES = 768
NY, NZ = 8, 12
NX = 4
ROWS = DEVICES * SPAN
HALF = ROWS // 2
NODE_ROWS = 30
PAD_ROWS = 32
BLOCKS = D // QBLK
STEP_BLOCKS = 16
STEPS = BLOCKS // STEP_BLOCKS
WIDTH = STEP_BLOCKS * QBLK
SWAP = [(0, 1), (1, 0)]
OPPOSITE = [(x * 2 + c, (x + (1 if (x + c) % 2 == 0 else -1)) % NX * 2 + c) for x in range(NX) for c in range(2)]
ALL = ("y", "z", "xh", "xl", "core")
PLANE = ("y", "xh", "xl")


def read_columns(source, target, sems, chunk):
    columns = pl.ds(chunk * WIDTH, WIDTH)
    return pltpu.make_async_copy(source.at[:, columns], target.at[:, columns], sems.at[chunk])


def dequant_kernel(codes_hbm, scales_hbm, out_hbm, codes, scales, out, scale_sem, read_sems, write_sems):
    scale_read = pltpu.make_async_copy(scales_hbm, scales, scale_sem)
    scale_read.start()
    for chunk in range(STEPS):
        read_columns(codes_hbm, codes, read_sems, chunk).start()
    scale_read.wait()
    fill = jnp.zeros((PAD_ROWS - NODE_ROWS, WIDTH), jnp.float32)
    for chunk in range(STEPS):
        columns = slice(chunk * WIDTH, (chunk + 1) * WIDTH)
        block_of = lax.broadcasted_iota(jnp.int32, (BLOCKS, WIDTH), 1) // QBLK + chunk * STEP_BLOCKS
        one_hot = (lax.broadcasted_iota(jnp.int32, (BLOCKS, WIDTH), 0) == block_of).astype(jnp.float32)
        wide = jnp.dot(scales[...], one_hot.astype(jnp.bfloat16), preferred_element_type=jnp.float32)
        read_columns(codes_hbm, codes, read_sems, chunk).wait()
        weight = codes[:, columns].astype(jnp.float32) * wide
        out[:, columns] = jnp.concatenate([weight, fill], axis=0).astype(jnp.bfloat16)
        read_columns(out, out_hbm, write_sems, chunk).start()
    for chunk in range(STEPS):
        read_columns(out, out_hbm, write_sems, chunk).wait()


def dequant(codes, scales):
    hbm = pl.BlockSpec(memory_space=pltpu.HBM)
    return pl.pallas_call(
        dequant_kernel,
        in_specs=[hbm, hbm],
        out_specs=hbm,
        scratch_shapes=[
            pltpu.VMEM((NODE_ROWS, D), jnp.bfloat16),
            pltpu.VMEM((NODE_ROWS, BLOCKS), jnp.bfloat16),
            pltpu.VMEM((PAD_ROWS, D), jnp.bfloat16),
            pltpu.SemaphoreType.DMA,
            pltpu.SemaphoreType.DMA((STEPS,)),
            pltpu.SemaphoreType.DMA((STEPS,)),
        ],
        out_shape=jax.ShapeDtypeStruct((PAD_ROWS, D), jnp.bfloat16),
        compiler_params=pltpu.CompilerParams(vmem_limit_bytes=56 * 2**20),
        cost_estimate=pl.CostEstimate(flops=PAD_ROWS * D, bytes_accessed=4 * PAD_ROWS * D, transcendentals=0),
    )(codes, scales)


def partial_kernel(
    core_ref, order_hbm, gate_up_hbm, out_grad_hbm, keep_ref, send_ref, order, gate_up, out_grad, blocks, staged, sems, small_sems
):
    small = [
        pltpu.make_async_copy(source, target, small_sems.at[i])
        for i, (source, target) in enumerate(
            ((gate_up_hbm, gate_up), (order_hbm, order))
        )
    ]
    small[0].start()
    for chunk in range(STEPS):
        read_columns(out_grad_hbm, out_grad, sems, chunk).start()
    small[1].start()
    small[0].wait()
    both = gate_up[...].astype(jnp.float32)
    gate, up = both[:FW], both[FW:]
    hidden = (gate * jax.nn.sigmoid(gate) * up).astype(jnp.bfloat16)
    for chunk in range(STEPS):
        columns = slice(chunk * WIDTH, (chunk + 1) * WIDTH)
        read_columns(out_grad_hbm, out_grad, sems, chunk).wait()
        product = jnp.dot(hidden, out_grad[:, columns], preferred_element_type=jnp.float32)
        for block in range(STEP_BLOCKS):
            blocks[pl.ds(chunk * STEP_BLOCKS + block, FW, stride=BLOCKS), :] = product[:, block * QBLK : (block + 1) * QBLK]
    small[1].wait()
    core = core_ref[0]
    first = (core * HALF, (1 - core) * HALF)

    def gather(y, carry):
        for z in range(NZ):
            for low in range(8):
                span = order[y * (8 * NZ) + z * 8 + low]
                place = first[low % 2] + y * (NX * NZ * SPAN) + ((low // 2) * NZ + z) * SPAN
                staged[pl.ds(place, SPAN), :] = blocks[pl.ds(span * SPAN, SPAN), :]
        return carry

    lax.fori_loop(0, NY, gather, 0)
    keep_ref[...] = staged[:HALF, :].astype(jnp.bfloat16)
    send_ref[...] = staged[HALF:, :].astype(jnp.bfloat16)


def partial_spans(order, core, gate_up_t, out_grad):
    hbm = pl.BlockSpec(memory_space=pltpu.HBM)
    vmem = pl.BlockSpec(memory_space=pltpu.VMEM)
    return pl.pallas_call(
        partial_kernel,
        in_specs=[pl.BlockSpec(memory_space=pltpu.SMEM)] + [hbm] * 3,
        out_specs=[vmem, vmem],
        scratch_shapes=[
            pltpu.SMEM((DEVICES,), jnp.int32),
            pltpu.VMEM((2 * FW, TOK), jnp.bfloat16),
            pltpu.VMEM((TOK, D), jnp.bfloat16),
            pltpu.VMEM((ROWS, QBLK), jnp.float32),
            pltpu.VMEM((ROWS, QBLK), jnp.float32),
            pltpu.SemaphoreType.DMA((STEPS,)),
            pltpu.SemaphoreType.DMA((2,)),
        ],
        out_shape=[
            jax.ShapeDtypeStruct((HALF, QBLK), jnp.bfloat16),
            jax.ShapeDtypeStruct((HALF, QBLK), jnp.bfloat16),
        ],
        compiler_params=pltpu.CompilerParams(vmem_limit_bytes=56 * 2**20),
        cost_estimate=pl.CostEstimate(flops=2 * FW * TOK * D, bytes_accessed=6 * (2 * TOK * D + 4 * HALF * QBLK) // 2, transcendentals=FW * TOK),
    )(core, order, gate_up_t, out_grad)


def grads_kernel(place_ref, gate_up_ref, own_hbm, core_hbm, x_hbm, both_hbm, out_grad_hbm, out_ref, weight, out_grad, weight_sems, sems):
    reads = []
    for i, part in enumerate((own_hbm, core_hbm, x_hbm, both_hbm)):
        row = pl.multiple_of(jnp.bitwise_xor(place_ref[0], i) * PAD_ROWS, PAD_ROWS)
        reads.append(pltpu.make_async_copy(part, weight.at[pl.ds(row, PAD_ROWS), :], weight_sems.at[i]))
        reads[-1].start()
    for chunk in range(STEPS):
        read_columns(out_grad_hbm, out_grad, sems, chunk).start()
    both = gate_up_ref[...].astype(jnp.float32)
    gate, up = both[:FW], both[FW:]
    sig = jax.nn.sigmoid(gate)
    for read in reads:
        read.wait()
    total = jnp.zeros((TOK, 4 * PAD_ROWS), jnp.float32)
    for chunk in range(STEPS):
        columns = slice(chunk * WIDTH, (chunk + 1) * WIDTH)
        read_columns(out_grad_hbm, out_grad, sems, chunk).wait()
        total += lax.dot_general(
            out_grad[:, columns], weight[:, columns], (((1,), (1,)), ((), ())), preferred_element_type=jnp.float32
        )
    total = total.T
    hidden_grad = jnp.concatenate([total[i * PAD_ROWS : i * PAD_ROWS + NODE_ROWS, :] for i in range(4)], axis=0)
    gate_grad = hidden_grad * up * sig * (1.0 + gate * (1.0 - sig))
    up_grad = hidden_grad * (gate * sig)
    out_ref[...] = jnp.concatenate([gate_grad, up_grad], axis=0).astype(jnp.bfloat16)


def input_grads(place, gate_up_t, parts, out_grad):
    smem = pl.BlockSpec(memory_space=pltpu.SMEM)
    vmem = pl.BlockSpec(memory_space=pltpu.VMEM)
    anywhere = pl.BlockSpec(memory_space=pl.ANY)
    return pl.pallas_call(
        grads_kernel,
        in_specs=[smem, vmem] + [anywhere] * 4 + [pl.BlockSpec(memory_space=pltpu.HBM)],
        out_specs=vmem,
        scratch_shapes=[
            pltpu.VMEM((4 * PAD_ROWS, D), jnp.bfloat16),
            pltpu.VMEM((TOK, D), jnp.bfloat16),
            pltpu.SemaphoreType.DMA((4,)),
            pltpu.SemaphoreType.DMA((STEPS,)),
        ],
        out_shape=jax.ShapeDtypeStruct((2 * FW, TOK), jnp.bfloat16),
        compiler_params=pltpu.CompilerParams(vmem_limit_bytes=56 * 2**20),
        cost_estimate=pl.CostEstimate(flops=2 * FW * TOK * D, bytes_accessed=2 * TOK * D + 2 * 128 * D, transcendentals=FW * TOK),
    )(place, gate_up_t, *parts, out_grad)


def plane_sum_kernel(got_ref, out_ref):
    rows = 2 * NZ * SPAN
    total = got_ref[:rows, :].astype(jnp.float32)
    for i in range(1, HALF // rows):
        total += got_ref[i * rows : (i + 1) * rows, :].astype(jnp.float32)
    out_ref[...] = (total[: rows // 2] + total[rows // 2 :]).astype(jnp.bfloat16)


def plane_sum(got):
    return pl.pallas_call(
        plane_sum_kernel,
        in_specs=[pl.BlockSpec(memory_space=pltpu.VMEM)],
        out_specs=pl.BlockSpec(memory_space=pltpu.VMEM),
        out_shape=jax.ShapeDtypeStruct((NZ * SPAN, QBLK), jnp.bfloat16),
        compiler_params=pltpu.CompilerParams(vmem_limit_bytes=4 * 2**20),
    )(got)


def last_sum_kernel(got_ref, out_ref, spans):
    spans[...] = got_ref[...].astype(jnp.float32)
    span = spans[:SPAN, :]
    for i in range(1, NZ):
        span += spans[i * SPAN : (i + 1) * SPAN, :]
    span = span * (1.0 / DEVICES)
    for i in range(SPAN):
        out_ref[:, i * QBLK : (i + 1) * QBLK] = span[i : i + 1, :]


def last_sum(got):
    return pl.pallas_call(
        last_sum_kernel,
        in_specs=[pl.BlockSpec(memory_space=pltpu.VMEM)],
        out_specs=pl.BlockSpec(memory_space=pltpu.VMEM),
        out_shape=jax.ShapeDtypeStruct((1, SPAN * QBLK), jnp.float32),
        scratch_shapes=[pltpu.VMEM((NZ * SPAN, QBLK), jnp.float32)],
        compiler_params=pltpu.CompilerParams(vmem_limit_bytes=2 * 2**20),
    )(got)


def per_device(gate_up, out_grad, weight_codes, weight_scales, shard_order):
    gate_up_t = gate_up.T
    core = lax.axis_index("core").astype(jnp.int32).reshape(1)
    place = lax.axis_index(("xl", "core")).astype(jnp.int32).reshape(1)
    weight = dequant(weight_codes, weight_scales)
    weight, gate_up_first = lax.optimization_barrier((weight, gate_up_t))
    weight_x = lax.ppermute(weight, ("xh", "xl", "core"), OPPOSITE)
    keep, send = partial_spans(shard_order, core, gate_up_first, out_grad)
    weight_x, weight, send = lax.optimization_barrier((weight_x, weight, send))
    got = lax.ppermute(send, "core", SWAP)
    pair = (keep.astype(jnp.float32) + got.astype(jnp.float32)).astype(jnp.bfloat16)
    got = lax.all_to_all(pair, PLANE, split_axis=0, concat_axis=0, tiled=True)
    weight_core = lax.ppermute(weight, "core", SWAP)
    weight_both = lax.ppermute(weight_x, "core", SWAP)
    grads = input_grads(place, gate_up_t, (weight, weight_core, weight_x, weight_both), out_grad)
    got, grads = lax.optimization_barrier((got, grads))
    line = plane_sum(got).reshape(NZ * SPAN // 2, 2, QBLK)
    got = lax.all_to_all(line, "z", split_axis=0, concat_axis=0, tiled=True)
    weight_grad = last_sum(got.reshape(NZ * SPAN, QBLK))
    return (grads.T, weight_grad)


def solution(mesh):
    fine = Mesh(mesh.devices.reshape(NY, NZ, 2, 2, 2), ALL)
    return jax.shard_map(
        per_device,
        mesh=fine,
        in_specs=(P(ALL, None), P(ALL, None), P(("xl", "core"), None), P(("xl", "core"), None), P()),
        out_specs=(P(ALL, None), P(ALL, None)),
        check_vma=False,
    )
```

```python
import jax
import jax.numpy as jnp
from jax import lax
from jax.experimental import pallas as pl
from jax.experimental.pallas import tpu as pltpu
from jax.sharding import Mesh
from jax.sharding import PartitionSpec as P

D = 8192
FW = 120
TOK = 256
QBLK = 128
SPAN = 10
DEVICES = 768
NY, NZ = 8, 12
NX = 4
ROWS = DEVICES * SPAN
HALF = ROWS // 2
NODE_ROWS = 30
PAD_ROWS = 32
BLOCKS = D // QBLK
STEP_BLOCKS = 16
STEPS = BLOCKS // STEP_BLOCKS
WIDTH = STEP_BLOCKS * QBLK
SWAP = [(0, 1), (1, 0)]
OPPOSITE = [(x * 2 + c, (x + (1 if (x + c) % 2 == 0 else -1)) % NX * 2 + c) for x in range(NX) for c in range(2)]
ALL = ("y", "z", "xh", "xl", "core")
PLANE = ("y", "xh", "xl")


def read_columns(source, target, sems, chunk):
    columns = pl.ds(chunk * WIDTH, WIDTH)
    return pltpu.make_async_copy(source.at[:, columns], target.at[:, columns], sems.at[chunk])


def partial_kernel(
    core_ref, order_hbm, gate_up_hbm, out_grad_hbm, codes_hbm, scales_hbm, keep_ref, send_ref, weight_ref,
    order, gate_up, codes, scales, out_grad, blocks, staged, sems, small_sems,
):
    small = [
        pltpu.make_async_copy(source, target, small_sems.at[i])
        for i, (source, target) in enumerate(
            ((gate_up_hbm, gate_up), (scales_hbm, scales), (codes_hbm, codes), (order_hbm, order))
        )
    ]
    small[0].start()
    for chunk in range(STEPS):
        read_columns(out_grad_hbm, out_grad, sems, chunk).start()
    for read in small[1:]:
        read.start()
    small[0].wait()
    both = gate_up[...].astype(jnp.float32)
    gate, up = both[:FW], both[FW:]
    hidden = (gate * jax.nn.sigmoid(gate) * up).astype(jnp.bfloat16)
    for chunk in range(STEPS):
        columns = slice(chunk * WIDTH, (chunk + 1) * WIDTH)
        read_columns(out_grad_hbm, out_grad, sems, chunk).wait()
        product = jnp.dot(hidden, out_grad[:, columns], preferred_element_type=jnp.float32)
        for block in range(STEP_BLOCKS):
            blocks[pl.ds(chunk * STEP_BLOCKS + block, FW, stride=BLOCKS), :] = product[:, block * QBLK : (block + 1) * QBLK]
    for read in small[1:]:
        read.wait()
    fill = jnp.zeros((PAD_ROWS - NODE_ROWS, WIDTH), jnp.float32)
    for chunk in range(STEPS):
        columns = slice(chunk * WIDTH, (chunk + 1) * WIDTH)
        block_of = lax.broadcasted_iota(jnp.int32, (BLOCKS, WIDTH), 1) // QBLK + chunk * STEP_BLOCKS
        one_hot = (lax.broadcasted_iota(jnp.int32, (BLOCKS, WIDTH), 0) == block_of).astype(jnp.float32)
        wide = jnp.dot(scales[...], one_hot.astype(jnp.bfloat16), preferred_element_type=jnp.float32)
        weight = codes[:, columns].astype(jnp.float32) * wide
        weight_ref[:, columns] = jnp.concatenate([weight, fill], axis=0).astype(jnp.bfloat16)

    core = core_ref[0]
    first = (core * HALF, (1 - core) * HALF)

    def gather(y, carry):
        for z in range(NZ):
            for low in range(8):
                span = order[y * (8 * NZ) + z * 8 + low]
                place = first[low % 2] + y * (NX * NZ * SPAN) + ((low // 2) * NZ + z) * SPAN
                staged[pl.ds(place, SPAN), :] = blocks[pl.ds(span * SPAN, SPAN), :]
        return carry

    lax.fori_loop(0, NY, gather, 0)
    keep_ref[...] = staged[:HALF, :].astype(jnp.bfloat16)
    send_ref[...] = staged[HALF:, :].astype(jnp.bfloat16)


def partial_spans(order, core, gate_up_t, out_grad, codes, scales):
    hbm = pl.BlockSpec(memory_space=pltpu.HBM)
    vmem = pl.BlockSpec(memory_space=pltpu.VMEM)
    return pl.pallas_call(
        partial_kernel,
        in_specs=[pl.BlockSpec(memory_space=pltpu.SMEM)] + [hbm] * 5,
        out_specs=[vmem, vmem, vmem],
        scratch_shapes=[
            pltpu.SMEM((DEVICES,), jnp.int32),
            pltpu.VMEM((2 * FW, TOK), jnp.bfloat16),
            pltpu.VMEM((NODE_ROWS, D), jnp.bfloat16),
            pltpu.VMEM((NODE_ROWS, BLOCKS), jnp.bfloat16),
            pltpu.VMEM((TOK, D), jnp.bfloat16),
            pltpu.VMEM((ROWS, QBLK), jnp.float32),
            pltpu.VMEM((ROWS, QBLK), jnp.float32),
            pltpu.SemaphoreType.DMA((STEPS,)),
            pltpu.SemaphoreType.DMA((4,)),
        ],
        out_shape=[
            jax.ShapeDtypeStruct((HALF, QBLK), jnp.bfloat16),
            jax.ShapeDtypeStruct((HALF, QBLK), jnp.bfloat16),
            jax.ShapeDtypeStruct((PAD_ROWS, D), jnp.bfloat16),
        ],
        compiler_params=pltpu.CompilerParams(vmem_limit_bytes=56 * 2**20),
        cost_estimate=pl.CostEstimate(flops=2 * FW * TOK * D, bytes_accessed=2 * TOK * D + 4 * HALF * QBLK, transcendentals=FW * TOK),
    )(core, order, gate_up_t, out_grad, codes, scales)


def grads_kernel(place_ref, gate_up_ref, own_hbm, core_hbm, x_hbm, both_hbm, out_grad_hbm, out_ref, weight, out_grad, weight_sems, sems):
    reads = []
    for i, part in enumerate((own_hbm, core_hbm, x_hbm, both_hbm)):
        row = pl.multiple_of(jnp.bitwise_xor(place_ref[0], i) * PAD_ROWS, PAD_ROWS)
        reads.append(pltpu.make_async_copy(part, weight.at[pl.ds(row, PAD_ROWS), :], weight_sems.at[i]))
        reads[-1].start()
    for chunk in range(STEPS):
        read_columns(out_grad_hbm, out_grad, sems, chunk).start()
    both = gate_up_ref[...].astype(jnp.float32)
    gate, up = both[:FW], both[FW:]
    sig = jax.nn.sigmoid(gate)
    for read in reads:
        read.wait()
    total = jnp.zeros((TOK, 4 * PAD_ROWS), jnp.float32)
    for chunk in range(STEPS):
        columns = slice(chunk * WIDTH, (chunk + 1) * WIDTH)
        read_columns(out_grad_hbm, out_grad, sems, chunk).wait()
        total += lax.dot_general(
            out_grad[:, columns], weight[:, columns], (((1,), (1,)), ((), ())), preferred_element_type=jnp.float32
        )
    total = total.T
    hidden_grad = jnp.concatenate([total[i * PAD_ROWS : i * PAD_ROWS + NODE_ROWS, :] for i in range(4)], axis=0)
    gate_grad = hidden_grad * up * sig * (1.0 + gate * (1.0 - sig))
    up_grad = hidden_grad * (gate * sig)
    out_ref[...] = jnp.concatenate([gate_grad, up_grad], axis=0).astype(jnp.bfloat16)


def input_grads(place, gate_up_t, parts, out_grad):
    smem = pl.BlockSpec(memory_space=pltpu.SMEM)
    vmem = pl.BlockSpec(memory_space=pltpu.VMEM)
    anywhere = pl.BlockSpec(memory_space=pl.ANY)
    return pl.pallas_call(
        grads_kernel,
        in_specs=[smem, vmem] + [anywhere] * 4 + [pl.BlockSpec(memory_space=pltpu.HBM)],
        out_specs=vmem,
        scratch_shapes=[
            pltpu.VMEM((4 * PAD_ROWS, D), jnp.bfloat16),
            pltpu.VMEM((TOK, D), jnp.bfloat16),
            pltpu.SemaphoreType.DMA((4,)),
            pltpu.SemaphoreType.DMA((STEPS,)),
        ],
        out_shape=jax.ShapeDtypeStruct((2 * FW, TOK), jnp.bfloat16),
        compiler_params=pltpu.CompilerParams(vmem_limit_bytes=56 * 2**20),
        cost_estimate=pl.CostEstimate(flops=2 * FW * TOK * D, bytes_accessed=2 * TOK * D + 2 * 128 * D, transcendentals=FW * TOK),
    )(place, gate_up_t, *parts, out_grad)


def plane_sum_kernel(got_ref, out_ref):
    rows = 2 * NZ * SPAN
    total = got_ref[:rows, :].astype(jnp.float32)
    for i in range(1, HALF // rows):
        total += got_ref[i * rows : (i + 1) * rows, :].astype(jnp.float32)
    out_ref[...] = (total[: rows // 2] + total[rows // 2 :]).astype(jnp.bfloat16)


def plane_sum(got):
    return pl.pallas_call(
        plane_sum_kernel,
        in_specs=[pl.BlockSpec(memory_space=pltpu.VMEM)],
        out_specs=pl.BlockSpec(memory_space=pltpu.VMEM),
        out_shape=jax.ShapeDtypeStruct((NZ * SPAN, QBLK), jnp.bfloat16),
        compiler_params=pltpu.CompilerParams(vmem_limit_bytes=4 * 2**20),
    )(got)


def last_sum_kernel(got_ref, out_ref, spans):
    spans[...] = got_ref[...].astype(jnp.float32)
    span = spans[:SPAN, :]
    for i in range(1, NZ):
        span += spans[i * SPAN : (i + 1) * SPAN, :]
    span = span * (1.0 / DEVICES)
    for i in range(SPAN):
        out_ref[:, i * QBLK : (i + 1) * QBLK] = span[i : i + 1, :]


def last_sum(got):
    return pl.pallas_call(
        last_sum_kernel,
        in_specs=[pl.BlockSpec(memory_space=pltpu.VMEM)],
        out_specs=pl.BlockSpec(memory_space=pltpu.VMEM),
        out_shape=jax.ShapeDtypeStruct((1, SPAN * QBLK), jnp.float32),
        scratch_shapes=[pltpu.VMEM((NZ * SPAN, QBLK), jnp.float32)],
        compiler_params=pltpu.CompilerParams(vmem_limit_bytes=2 * 2**20),
    )(got)


def per_device(gate_up, out_grad, weight_codes, weight_scales, shard_order):
    gate_up_t = gate_up.T
    core = lax.axis_index("core").astype(jnp.int32).reshape(1)
    place = lax.axis_index(("xl", "core")).astype(jnp.int32).reshape(1)
    keep, send, weight = partial_spans(shard_order, core, gate_up_t, out_grad, weight_codes, weight_scales)
    got = lax.ppermute(send, "core", SWAP)
    weight_x = lax.ppermute(weight, ("xh", "xl", "core"), OPPOSITE)
    pair = (keep.astype(jnp.float32) + got.astype(jnp.float32)).astype(jnp.bfloat16)
    weight_x, weight, pair = lax.optimization_barrier((weight_x, weight, pair))
    got = lax.all_to_all(pair, PLANE, split_axis=0, concat_axis=0, tiled=True)
    line = plane_sum(got)
    weight_x, weight, line = lax.optimization_barrier((weight_x, weight, line))
    weight_core = lax.ppermute(weight, "core", SWAP)
    weight_both = lax.ppermute(weight_x, "core", SWAP)
    got = lax.all_to_all(line.reshape(NZ * SPAN // 2, 2, QBLK), "z", split_axis=0, concat_axis=0, tiled=True)
    grads = input_grads(place, gate_up_t, (weight, weight_core, weight_x, weight_both), out_grad)
    got, grads = lax.optimization_barrier((got, grads))
    weight_grad = last_sum(got.reshape(NZ * SPAN, QBLK))
    return (grads.T, weight_grad)


def solution(mesh):
    fine = Mesh(mesh.devices.reshape(NY, NZ, 2, 2, 2), ALL)
    return jax.shard_map(
        per_device,
        mesh=fine,
        in_specs=(P(ALL, None), P(ALL, None), P(("xl", "core"), None), P(("xl", "core"), None), P()),
        out_specs=(P(ALL, None), P(ALL, None)),
        check_vma=False,
    )
```

```python
import jax
import jax.numpy as jnp
from jax import lax
from jax.experimental import pallas as pl
from jax.experimental.pallas import tpu as pltpu
from jax.sharding import Mesh
from jax.sharding import PartitionSpec as P

D = 8192
FW = 120
TOK = 256
QBLK = 128
SPAN = 10
DEVICES = 768
NY, NZ = 8, 12
NX = 4
ROWS = DEVICES * SPAN
HALF = ROWS // 2
NODE_ROWS = 30
PAD_ROWS = 32
BLOCKS = D // QBLK
STEP_BLOCKS = 16
STEPS = BLOCKS // STEP_BLOCKS
WIDTH = STEP_BLOCKS * QBLK
SWAP = [(0, 1), (1, 0)]
FIRST = [(x * 2 + c, (x + (1 if (x + c) % 2 == 0 else -1)) % NX * 2 + c) for x in range(NX) for c in range(2)]
SECOND = [(x * 2 + c, (x + (-1 if (x + c) % 2 == 0 else 1)) % NX * 2 + c) for x in range(NX) for c in range(2)]
XROWS = HALF // NX
ALL = ("y", "z", "xh", "xl", "core")
XC = ("xh", "xl", "core")


def read_columns(source, target, sems, chunk):
    columns = pl.ds(chunk * WIDTH, WIDTH)
    return pltpu.make_async_copy(source.at[:, columns], target.at[:, columns], sems.at[chunk])


def partial_kernel(
    core_ref, x_ref, order_hbm, gate_up_hbm, out_grad_hbm, codes_hbm, scales_hbm, keep_ref, send_ref, weight_ref,
    order, gate_up, codes, scales, out_grad, blocks, staged, sems, small_sems,
):
    small = [
        pltpu.make_async_copy(source, target, small_sems.at[i])
        for i, (source, target) in enumerate(
            ((gate_up_hbm, gate_up), (scales_hbm, scales), (codes_hbm, codes), (order_hbm, order))
        )
    ]
    small[0].start()
    for chunk in range(STEPS):
        read_columns(out_grad_hbm, out_grad, sems, chunk).start()
    for read in small[1:]:
        read.start()
    small[0].wait()
    both = gate_up[...].astype(jnp.float32)
    gate, up = both[:FW], both[FW:]
    hidden = (gate * jax.nn.sigmoid(gate) * up).astype(jnp.bfloat16)
    for chunk in range(STEPS):
        columns = slice(chunk * WIDTH, (chunk + 1) * WIDTH)
        read_columns(out_grad_hbm, out_grad, sems, chunk).wait()
        product = jnp.dot(hidden, out_grad[:, columns], preferred_element_type=jnp.float32)
        for block in range(STEP_BLOCKS):
            blocks[pl.ds(chunk * STEP_BLOCKS + block, FW, stride=BLOCKS), :] = product[:, block * QBLK : (block + 1) * QBLK]
    for read in small[1:]:
        read.wait()
    fill = jnp.zeros((PAD_ROWS - NODE_ROWS, WIDTH), jnp.float32)
    for chunk in range(STEPS):
        columns = slice(chunk * WIDTH, (chunk + 1) * WIDTH)
        block_of = lax.broadcasted_iota(jnp.int32, (BLOCKS, WIDTH), 1) // QBLK + chunk * STEP_BLOCKS
        one_hot = (lax.broadcasted_iota(jnp.int32, (BLOCKS, WIDTH), 0) == block_of).astype(jnp.float32)
        wide = jnp.dot(scales[...], one_hot.astype(jnp.bfloat16), preferred_element_type=jnp.float32)
        weight = codes[:, columns].astype(jnp.float32) * wide
        weight_ref[:, columns] = jnp.concatenate([weight, fill], axis=0).astype(jnp.bfloat16)

    core, x = core_ref[0], x_ref[0]
    bases = []
    for low in range(8):
        owner_x, owner_core = low // 2, low % 2
        away = (owner_x - x) & (NX - 1)
        ahead_first = ((x + owner_core) & 1) == 0
        beside = jnp.where((away == 1) == ahead_first, 2, 1)
        slot = jnp.where(away == 0, 0, jnp.where(away == 2, 3, beside))
        bases.append(jnp.where(core == owner_core, 0, HALF) + slot * XROWS)

    def gather(yz, carry):
        for low in range(8):
            span = order[yz * 8 + low]
            staged[pl.ds(bases[low] + yz * SPAN, SPAN), :] = blocks[pl.ds(span * SPAN, SPAN), :]
        return carry

    lax.fori_loop(0, NY * NZ, gather, 0, unroll=4)
    keep_ref[...] = staged[:HALF, :].astype(jnp.bfloat16)
    send_ref[...] = staged[HALF:, :].astype(jnp.bfloat16)


def partial_spans(order, core, x, gate_up_t, out_grad, codes, scales):
    hbm = pl.BlockSpec(memory_space=pltpu.HBM)
    vmem = pl.BlockSpec(memory_space=pltpu.VMEM)
    return pl.pallas_call(
        partial_kernel,
        in_specs=[pl.BlockSpec(memory_space=pltpu.SMEM)] * 2 + [hbm] * 5,
        out_specs=[vmem, vmem, vmem],
        scratch_shapes=[
            pltpu.SMEM((DEVICES,), jnp.int32),
            pltpu.VMEM((2 * FW, TOK), jnp.bfloat16),
            pltpu.VMEM((NODE_ROWS, D), jnp.bfloat16),
            pltpu.VMEM((NODE_ROWS, BLOCKS), jnp.bfloat16),
            pltpu.VMEM((TOK, D), jnp.bfloat16),
            pltpu.VMEM((ROWS, QBLK), jnp.float32),
            pltpu.VMEM((ROWS, QBLK), jnp.float32),
            pltpu.SemaphoreType.DMA((STEPS,)),
            pltpu.SemaphoreType.DMA((4,)),
        ],
        out_shape=[
            jax.ShapeDtypeStruct((HALF, QBLK), jnp.bfloat16),
            jax.ShapeDtypeStruct((HALF, QBLK), jnp.bfloat16),
            jax.ShapeDtypeStruct((PAD_ROWS, D), jnp.bfloat16),
        ],
        compiler_params=pltpu.CompilerParams(vmem_limit_bytes=56 * 2**20),
        cost_estimate=pl.CostEstimate(flops=2 * FW * TOK * D, bytes_accessed=2 * TOK * D + 4 * HALF * QBLK, transcendentals=FW * TOK),
    )(core, x, order, gate_up_t, out_grad, codes, scales)


def grads_kernel(place_ref, gate_up_ref, own_hbm, core_hbm, x_hbm, both_hbm, out_grad_hbm, out_ref, weight, out_grad, weight_sems, sems):
    reads = []
    for i, part in enumerate((own_hbm, core_hbm, x_hbm, both_hbm)):
        row = pl.multiple_of(jnp.bitwise_xor(place_ref[0], i) * PAD_ROWS, PAD_ROWS)
        reads.append(pltpu.make_async_copy(part, weight.at[pl.ds(row, PAD_ROWS), :], weight_sems.at[i]))
        reads[-1].start()
    for chunk in range(STEPS):
        read_columns(out_grad_hbm, out_grad, sems, chunk).start()
    both = gate_up_ref[...].astype(jnp.float32)
    gate, up = both[:FW], both[FW:]
    sig = jax.nn.sigmoid(gate)
    for read in reads:
        read.wait()
    total = jnp.zeros((TOK, 4 * PAD_ROWS), jnp.float32)
    for chunk in range(STEPS):
        columns = slice(chunk * WIDTH, (chunk + 1) * WIDTH)
        read_columns(out_grad_hbm, out_grad, sems, chunk).wait()
        total += lax.dot_general(
            out_grad[:, columns], weight[:, columns], (((1,), (1,)), ((), ())), preferred_element_type=jnp.float32
        )
    total = total.T
    hidden_grad = jnp.concatenate([total[i * PAD_ROWS : i * PAD_ROWS + NODE_ROWS, :] for i in range(4)], axis=0)
    gate_grad = hidden_grad * up * sig * (1.0 + gate * (1.0 - sig))
    up_grad = hidden_grad * (gate * sig)
    out_ref[...] = jnp.concatenate([gate_grad, up_grad], axis=0).astype(jnp.bfloat16)


def input_grads(place, gate_up_t, parts, out_grad):
    smem = pl.BlockSpec(memory_space=pltpu.SMEM)
    vmem = pl.BlockSpec(memory_space=pltpu.VMEM)
    anywhere = pl.BlockSpec(memory_space=pl.ANY)
    return pl.pallas_call(
        grads_kernel,
        in_specs=[smem, vmem] + [anywhere] * 4 + [pl.BlockSpec(memory_space=pltpu.HBM)],
        out_specs=vmem,
        scratch_shapes=[
            pltpu.VMEM((4 * PAD_ROWS, D), jnp.bfloat16),
            pltpu.VMEM((TOK, D), jnp.bfloat16),
            pltpu.SemaphoreType.DMA((4,)),
            pltpu.SemaphoreType.DMA((STEPS,)),
        ],
        out_shape=jax.ShapeDtypeStruct((2 * FW, TOK), jnp.bfloat16),
        compiler_params=pltpu.CompilerParams(vmem_limit_bytes=56 * 2**20),
        cost_estimate=pl.CostEstimate(flops=2 * FW * TOK * D, bytes_accessed=2 * TOK * D + 2 * 128 * D, transcendentals=FW * TOK),
    )(place, gate_up_t, *parts, out_grad)


def y_sum_kernel(got_ref, out_ref):
    rows = 2 * NZ * SPAN
    total = got_ref[:rows, :].astype(jnp.float32)
    for i in range(1, XROWS // rows):
        total += got_ref[i * rows : (i + 1) * rows, :].astype(jnp.float32)
    out_ref[...] = (total[: rows // 2] + total[rows // 2 :]).astype(jnp.bfloat16)


def y_sum(got):
    return pl.pallas_call(
        y_sum_kernel,
        in_specs=[pl.BlockSpec(memory_space=pltpu.VMEM)],
        out_specs=pl.BlockSpec(memory_space=pltpu.VMEM),
        out_shape=jax.ShapeDtypeStruct((NZ * SPAN, QBLK), jnp.bfloat16),
        compiler_params=pltpu.CompilerParams(vmem_limit_bytes=4 * 2**20),
    )(got)


def last_sum_kernel(got_ref, out_ref, spans):
    spans[...] = got_ref[...].astype(jnp.float32)
    span = spans[:SPAN, :]
    for i in range(1, NZ):
        span += spans[i * SPAN : (i + 1) * SPAN, :]
    span = span * (1.0 / DEVICES)
    for i in range(SPAN):
        out_ref[:, i * QBLK : (i + 1) * QBLK] = span[i : i + 1, :]


def last_sum(got):
    return pl.pallas_call(
        last_sum_kernel,
        in_specs=[pl.BlockSpec(memory_space=pltpu.VMEM)],
        out_specs=pl.BlockSpec(memory_space=pltpu.VMEM),
        out_shape=jax.ShapeDtypeStruct((1, SPAN * QBLK), jnp.float32),
        scratch_shapes=[pltpu.VMEM((NZ * SPAN, QBLK), jnp.float32)],
        compiler_params=pltpu.CompilerParams(vmem_limit_bytes=2 * 2**20),
    )(got)


def per_device(gate_up, out_grad, weight_codes, weight_scales, shard_order):
    gate_up_t = gate_up.T
    core = lax.axis_index("core").astype(jnp.int32).reshape(1)
    place = lax.axis_index(("xl", "core")).astype(jnp.int32).reshape(1)
    x = lax.axis_index(("xh", "xl")).astype(jnp.int32).reshape(1)
    keep, send, weight = partial_spans(shard_order, core, x, gate_up_t, out_grad, weight_codes, weight_scales)
    got = lax.ppermute(send, "core", SWAP)
    pair = lambda first, last: keep[first:last].astype(jnp.float32) + got[first:last].astype(jnp.float32)
    first_got = lax.ppermute(pair(2 * XROWS, 4 * XROWS).astype(jnp.bfloat16), XC, FIRST)
    second_send = (pair(XROWS, 2 * XROWS) + first_got[XROWS:].astype(jnp.float32)).astype(jnp.bfloat16)
    second_got = lax.ppermute(second_send, XC, SECOND).astype(jnp.float32)
    line = (pair(0, XROWS) + first_got[:XROWS].astype(jnp.float32) + second_got).astype(jnp.bfloat16)
    weight, line = lax.optimization_barrier((weight, line))
    weight_x = lax.ppermute(weight, XC, FIRST)
    weight_core = lax.ppermute(weight, "core", SWAP)
    got = y_sum(lax.all_to_all(line, "y", split_axis=0, concat_axis=0, tiled=True))
    weight_x, got = lax.optimization_barrier((weight_x, got))
    weight_both = lax.ppermute(weight_x, "core", SWAP)
    got = lax.all_to_all(got.reshape(NZ * SPAN // 2, 2, QBLK), "z", split_axis=0, concat_axis=0, tiled=True)
    grads = input_grads(place, gate_up_t, (weight, weight_core, weight_x, weight_both), out_grad)
    got, grads = lax.optimization_barrier((got, grads))
    weight_grad = last_sum(got.reshape(NZ * SPAN, QBLK))
    return (grads.T, weight_grad)


def solution(mesh):
    fine = Mesh(mesh.devices.reshape(NY, NZ, 2, 2, 2), ALL)
    return jax.shard_map(
        per_device,
        mesh=fine,
        in_specs=(P(ALL, None), P(ALL, None), P(("xl", "core"), None), P(("xl", "core"), None), P()),
        out_specs=(P(ALL, None), P(ALL, None)),
        check_vma=False,
    )
```

```python
import jax
import jax.numpy as jnp
from jax import lax
from jax.experimental import pallas as pl
from jax.experimental.pallas import tpu as pltpu
from jax.sharding import Mesh
from jax.sharding import PartitionSpec as P

D = 8192
FW = 120
TOK = 256
QBLK = 128
SPAN = 10
DEVICES = 768
NY, NZ = 8, 12
NX = 4
ROWS = DEVICES * SPAN
HALF = ROWS // 2
NODE_ROWS = 30
PAD_ROWS = 32
BLOCKS = D // QBLK
STEP_BLOCKS = 16
STEPS = BLOCKS // STEP_BLOCKS
WIDTH = STEP_BLOCKS * QBLK
SWAP = [(0, 1), (1, 0)]
OPPOSITE = [(x * 2 + c, (x + (1 if (x + c) % 2 == 0 else -1)) % NX * 2 + c) for x in range(NX) for c in range(2)]
XROWS = HALF // NX
ALL = ("y", "z", "xh", "xl", "core")
XC = ("xh", "xl", "core")


def read_columns(source, target, sems, chunk):
    columns = pl.ds(chunk * WIDTH, WIDTH)
    return pltpu.make_async_copy(source.at[:, columns], target.at[:, columns], sems.at[chunk])


def partial_kernel(
    core_ref, order_hbm, gate_up_hbm, out_grad_hbm, codes_hbm, scales_hbm, keep_ref, send_ref, weight_ref,
    order, gate_up, codes, scales, out_grad, blocks, staged, sems, small_sems,
):
    small = [
        pltpu.make_async_copy(source, target, small_sems.at[i])
        for i, (source, target) in enumerate(
            ((gate_up_hbm, gate_up), (scales_hbm, scales), (codes_hbm, codes), (order_hbm, order))
        )
    ]
    small[0].start()
    for chunk in range(STEPS):
        read_columns(out_grad_hbm, out_grad, sems, chunk).start()
    for read in small[1:]:
        read.start()
    small[0].wait()
    both = gate_up[...].astype(jnp.float32)
    gate, up = both[:FW], both[FW:]
    hidden = (gate * jax.nn.sigmoid(gate) * up).astype(jnp.bfloat16)
    for chunk in range(STEPS):
        columns = slice(chunk * WIDTH, (chunk + 1) * WIDTH)
        read_columns(out_grad_hbm, out_grad, sems, chunk).wait()
        product = jnp.dot(hidden, out_grad[:, columns], preferred_element_type=jnp.float32)
        for block in range(STEP_BLOCKS):
            blocks[pl.ds(chunk * STEP_BLOCKS + block, FW, stride=BLOCKS), :] = product[:, block * QBLK : (block + 1) * QBLK]
    for read in small[1:]:
        read.wait()
    fill = jnp.zeros((PAD_ROWS - NODE_ROWS, WIDTH), jnp.float32)
    for chunk in range(STEPS):
        columns = slice(chunk * WIDTH, (chunk + 1) * WIDTH)
        block_of = lax.broadcasted_iota(jnp.int32, (BLOCKS, WIDTH), 1) // QBLK + chunk * STEP_BLOCKS
        one_hot = (lax.broadcasted_iota(jnp.int32, (BLOCKS, WIDTH), 0) == block_of).astype(jnp.float32)
        wide = jnp.dot(scales[...], one_hot.astype(jnp.bfloat16), preferred_element_type=jnp.float32)
        weight = codes[:, columns].astype(jnp.float32) * wide
        weight_ref[:, columns] = jnp.concatenate([weight, fill], axis=0).astype(jnp.bfloat16)

    core = core_ref[0]
    first = (core * HALF, (1 - core) * HALF)

    def gather(yz, carry):
        for low in range(8):
            span = order[yz * 8 + low]
            place = first[low % 2] + (low // 2) * XROWS + yz * SPAN
            staged[pl.ds(place, SPAN), :] = blocks[pl.ds(span * SPAN, SPAN), :]
        return carry

    lax.fori_loop(0, NY * NZ, gather, 0, unroll=4)
    keep_ref[...] = staged[:HALF, :].astype(jnp.bfloat16)
    send_ref[...] = staged[HALF:, :].astype(jnp.bfloat16)


def partial_spans(order, core, gate_up_t, out_grad, codes, scales):
    hbm = pl.BlockSpec(memory_space=pltpu.HBM)
    vmem = pl.BlockSpec(memory_space=pltpu.VMEM)
    return pl.pallas_call(
        partial_kernel,
        in_specs=[pl.BlockSpec(memory_space=pltpu.SMEM)] + [hbm] * 5,
        out_specs=[vmem, vmem, vmem],
        scratch_shapes=[
            pltpu.SMEM((DEVICES,), jnp.int32),
            pltpu.VMEM((2 * FW, TOK), jnp.bfloat16),
            pltpu.VMEM((NODE_ROWS, D), jnp.bfloat16),
            pltpu.VMEM((NODE_ROWS, BLOCKS), jnp.bfloat16),
            pltpu.VMEM((TOK, D), jnp.bfloat16),
            pltpu.VMEM((ROWS, QBLK), jnp.float32),
            pltpu.VMEM((ROWS, QBLK), jnp.float32),
            pltpu.SemaphoreType.DMA((STEPS,)),
            pltpu.SemaphoreType.DMA((4,)),
        ],
        out_shape=[
            jax.ShapeDtypeStruct((HALF, QBLK), jnp.bfloat16),
            jax.ShapeDtypeStruct((HALF, QBLK), jnp.bfloat16),
            jax.ShapeDtypeStruct((PAD_ROWS, D), jnp.bfloat16),
        ],
        compiler_params=pltpu.CompilerParams(vmem_limit_bytes=56 * 2**20),
        cost_estimate=pl.CostEstimate(flops=2 * FW * TOK * D, bytes_accessed=2 * TOK * D + 4 * HALF * QBLK, transcendentals=FW * TOK),
    )(core, order, gate_up_t, out_grad, codes, scales)


def grads_kernel(place_ref, gate_up_ref, own_hbm, core_hbm, x_hbm, both_hbm, out_grad_hbm, out_ref, weight, out_grad, weight_sems, sems):
    reads = []
    for i, part in enumerate((own_hbm, core_hbm, x_hbm, both_hbm)):
        row = pl.multiple_of(jnp.bitwise_xor(place_ref[0], i) * PAD_ROWS, PAD_ROWS)
        reads.append(pltpu.make_async_copy(part, weight.at[pl.ds(row, PAD_ROWS), :], weight_sems.at[i]))
        reads[-1].start()
    for chunk in range(STEPS):
        read_columns(out_grad_hbm, out_grad, sems, chunk).start()
    both = gate_up_ref[...].astype(jnp.float32)
    gate, up = both[:FW], both[FW:]
    sig = jax.nn.sigmoid(gate)
    for read in reads:
        read.wait()
    total = jnp.zeros((TOK, 4 * PAD_ROWS), jnp.float32)
    for chunk in range(STEPS):
        columns = slice(chunk * WIDTH, (chunk + 1) * WIDTH)
        read_columns(out_grad_hbm, out_grad, sems, chunk).wait()
        total += lax.dot_general(
            out_grad[:, columns], weight[:, columns], (((1,), (1,)), ((), ())), preferred_element_type=jnp.float32
        )
    total = total.T
    hidden_grad = jnp.concatenate([total[i * PAD_ROWS : i * PAD_ROWS + NODE_ROWS, :] for i in range(4)], axis=0)
    gate_grad = hidden_grad * up * sig * (1.0 + gate * (1.0 - sig))
    up_grad = hidden_grad * (gate * sig)
    out_ref[...] = jnp.concatenate([gate_grad, up_grad], axis=0).astype(jnp.bfloat16)


def input_grads(place, gate_up_t, parts, out_grad):
    smem = pl.BlockSpec(memory_space=pltpu.SMEM)
    vmem = pl.BlockSpec(memory_space=pltpu.VMEM)
    anywhere = pl.BlockSpec(memory_space=pl.ANY)
    return pl.pallas_call(
        grads_kernel,
        in_specs=[smem, vmem] + [anywhere] * 4 + [pl.BlockSpec(memory_space=pltpu.HBM)],
        out_specs=vmem,
        scratch_shapes=[
            pltpu.VMEM((4 * PAD_ROWS, D), jnp.bfloat16),
            pltpu.VMEM((TOK, D), jnp.bfloat16),
            pltpu.SemaphoreType.DMA((4,)),
            pltpu.SemaphoreType.DMA((STEPS,)),
        ],
        out_shape=jax.ShapeDtypeStruct((2 * FW, TOK), jnp.bfloat16),
        compiler_params=pltpu.CompilerParams(vmem_limit_bytes=56 * 2**20),
        cost_estimate=pl.CostEstimate(flops=2 * FW * TOK * D, bytes_accessed=2 * TOK * D + 2 * 128 * D, transcendentals=FW * TOK),
    )(place, gate_up_t, *parts, out_grad)


def last_sum_kernel(got_ref, out_ref, total):
    rows = 8 * SPAN
    eight = got_ref[:rows, :].astype(jnp.float32)
    for i in range(1, XROWS // rows):
        eight += got_ref[i * rows : (i + 1) * rows, :].astype(jnp.float32)
    total[...] = eight
    span = total[:SPAN, :]
    for i in range(1, 8):
        span += total[i * SPAN : (i + 1) * SPAN, :]
    span = span * (1.0 / DEVICES)
    for i in range(SPAN):
        out_ref[:, i * QBLK : (i + 1) * QBLK] = span[i : i + 1, :]


def last_sum(got):
    return pl.pallas_call(
        last_sum_kernel,
        in_specs=[pl.BlockSpec(memory_space=pltpu.VMEM)],
        out_specs=pl.BlockSpec(memory_space=pltpu.VMEM),
        out_shape=jax.ShapeDtypeStruct((1, SPAN * QBLK), jnp.float32),
        scratch_shapes=[pltpu.VMEM((8 * SPAN, QBLK), jnp.float32)],
        compiler_params=pltpu.CompilerParams(vmem_limit_bytes=2 * 2**20),
    )(got)


def per_device(gate_up, out_grad, weight_codes, weight_scales, shard_order):
    gate_up_t = gate_up.T
    core = lax.axis_index("core").astype(jnp.int32).reshape(1)
    place = lax.axis_index(("xl", "core")).astype(jnp.int32).reshape(1)
    keep, send, weight = partial_spans(shard_order, core, gate_up_t, out_grad, weight_codes, weight_scales)
    got = lax.ppermute(send, "core", SWAP)
    pair = (keep.astype(jnp.float32) + got.astype(jnp.float32)).astype(jnp.bfloat16)
    got = lax.all_to_all(pair, ("xh", "xl"), split_axis=0, concat_axis=0, tiled=True)
    parts = [got[i * XROWS : (i + 1) * XROWS].astype(jnp.float32) for i in range(NX)]
    line = (parts[0] + parts[1] + parts[2] + parts[3]).astype(jnp.bfloat16)
    weight, line = lax.optimization_barrier((weight, line))
    weight_x = lax.ppermute(weight, XC, OPPOSITE)
    weight_core = lax.ppermute(weight, "core", SWAP)
    weight_both = lax.ppermute(weight_x, "core", SWAP)
    got = lax.all_to_all(line.reshape(XROWS // 2, 2, QBLK), ("y", "z"), split_axis=0, concat_axis=0, tiled=True)
    grads = input_grads(place, gate_up_t, (weight, weight_core, weight_x, weight_both), out_grad)
    got, grads = lax.optimization_barrier((got, grads))
    weight_grad = last_sum(got.reshape(XROWS, QBLK))
    return (grads.T, weight_grad)


def solution(mesh):
    fine = Mesh(mesh.devices.reshape(NY, NZ, 2, 2, 2), ALL)
    return jax.shard_map(
        per_device,
        mesh=fine,
        in_specs=(P(ALL, None), P(ALL, None), P(("xl", "core"), None), P(("xl", "core"), None), P()),
        out_specs=(P(ALL, None), P(ALL, None)),
        check_vma=False,
    )
```

```python
import jax
import jax.numpy as jnp
from jax import lax
from jax.experimental import pallas as pl
from jax.experimental.pallas import tpu as pltpu
from jax.sharding import Mesh
from jax.sharding import PartitionSpec as P

D = 8192
FW = 120
TOK = 256
QBLK = 128
SPAN = 10
DEVICES = 768
NY, NZ = 8, 12
NX = 4
ROWS = DEVICES * SPAN
HALF = ROWS // 2
NODE_ROWS = 30
PAD_ROWS = 32
BLOCKS = D // QBLK
STEP_BLOCKS = 16
STEPS = BLOCKS // STEP_BLOCKS
WIDTH = STEP_BLOCKS * QBLK
GRAD_STEPS = 2
GRAD_WIDTH = D // GRAD_STEPS
SWAP = [(0, 1), (1, 0)]
OPPOSITE = [(x * 2 + c, (x + (1 if (x + c) % 2 == 0 else -1)) % NX * 2 + c) for x in range(NX) for c in range(2)]
XROWS = HALF // NX
ALL = ("y", "z", "xh", "xl", "core")
XC = ("xh", "xl", "core")


def read_columns(source, target, sems, chunk, width=WIDTH):
    columns = pl.ds(chunk * width, width)
    return pltpu.make_async_copy(source.at[:, columns], target.at[:, columns], sems.at[chunk])


def partial_kernel(
    core_ref, order_hbm, gate_up_hbm, out_grad_hbm, codes_hbm, scales_hbm, keep_hbm, send_hbm, weight_hbm,
    order, gate_up, codes, scales, out_grad, blocks, staged, spans_out, weight_out, sems, small_sems, write_sems,
):
    small = [
        pltpu.make_async_copy(source, target, small_sems.at[i])
        for i, (source, target) in enumerate(
            ((gate_up_hbm, gate_up), (scales_hbm, scales), (codes_hbm, codes), (order_hbm, order))
        )
    ]
    small[0].start()
    for chunk in range(STEPS):
        read_columns(out_grad_hbm, out_grad, sems, chunk).start()
    for read in small[1:]:
        read.start()
    small[0].wait()
    both = gate_up[...].astype(jnp.float32)
    gate, up = both[:FW], both[FW:]
    hidden = (gate * jax.nn.sigmoid(gate) * up).astype(jnp.bfloat16)
    for chunk in range(STEPS):
        columns = slice(chunk * WIDTH, (chunk + 1) * WIDTH)
        read_columns(out_grad_hbm, out_grad, sems, chunk).wait()
        product = jnp.dot(hidden, out_grad[:, columns], preferred_element_type=jnp.float32)
        for block in range(STEP_BLOCKS):
            blocks[pl.ds(chunk * STEP_BLOCKS + block, FW, stride=BLOCKS), :] = product[:, block * QBLK : (block + 1) * QBLK]
    for read in small[1:]:
        read.wait()
    fill = jnp.zeros((PAD_ROWS - NODE_ROWS, WIDTH), jnp.float32)
    for chunk in range(STEPS):
        columns = slice(chunk * WIDTH, (chunk + 1) * WIDTH)
        block_of = lax.broadcasted_iota(jnp.int32, (BLOCKS, WIDTH), 1) // QBLK + chunk * STEP_BLOCKS
        one_hot = (lax.broadcasted_iota(jnp.int32, (BLOCKS, WIDTH), 0) == block_of).astype(jnp.float32)
        wide = jnp.dot(scales[...], one_hot.astype(jnp.bfloat16), preferred_element_type=jnp.float32)
        weight = codes[:, columns].astype(jnp.float32) * wide
        weight_out[:, columns] = jnp.concatenate([weight, fill], axis=0).astype(jnp.bfloat16)

    weight_write = pltpu.make_async_copy(weight_out, weight_hbm, write_sems.at[2 * NX])
    weight_write.start()
    core = core_ref[0]
    writes = [weight_write]
    for side, (owner_core, target) in enumerate(((core, keep_hbm), (1 - core, send_hbm))):
        for x in range(NX):
            rows = pl.ds(x * XROWS, XROWS)

            def gather(yz, carry):
                span = order[yz * 8 + x * 2 + owner_core]
                staged[pl.ds(yz * SPAN, SPAN), :] = blocks[pl.ds(span * SPAN, SPAN), :]
                return carry

            lax.fori_loop(0, NY * NZ, gather, 0, unroll=32)
            spans_out[side, rows, :] = staged[...].astype(jnp.bfloat16)
            write = pltpu.make_async_copy(spans_out.at[side, rows, :], target.at[rows, :], write_sems.at[side * NX + x])
            write.start()
            writes.append(write)
    for write in writes:
        write.wait()


def partial_spans(order, core, gate_up_t, out_grad, codes, scales):
    hbm = pl.BlockSpec(memory_space=pltpu.HBM)
    return pl.pallas_call(
        partial_kernel,
        in_specs=[pl.BlockSpec(memory_space=pltpu.SMEM)] + [hbm] * 5,
        out_specs=[hbm, hbm, hbm],
        scratch_shapes=[
            pltpu.SMEM((DEVICES,), jnp.int32),
            pltpu.VMEM((2 * FW, TOK), jnp.bfloat16),
            pltpu.VMEM((NODE_ROWS, D), jnp.bfloat16),
            pltpu.VMEM((NODE_ROWS, BLOCKS), jnp.bfloat16),
            pltpu.VMEM((TOK, D), jnp.bfloat16),
            pltpu.VMEM((ROWS, QBLK), jnp.float32),
            pltpu.VMEM((XROWS, QBLK), jnp.float32),
            pltpu.VMEM((2, HALF, QBLK), jnp.bfloat16),
            pltpu.VMEM((PAD_ROWS, D), jnp.bfloat16),
            pltpu.SemaphoreType.DMA((STEPS,)),
            pltpu.SemaphoreType.DMA((4,)),
            pltpu.SemaphoreType.DMA((2 * NX + 1,)),
        ],
        out_shape=[
            jax.ShapeDtypeStruct((HALF, QBLK), jnp.bfloat16),
            jax.ShapeDtypeStruct((HALF, QBLK), jnp.bfloat16),
            jax.ShapeDtypeStruct((PAD_ROWS, D), jnp.bfloat16),
        ],
        compiler_params=pltpu.CompilerParams(vmem_limit_bytes=56 * 2**20),
        cost_estimate=pl.CostEstimate(flops=2 * FW * TOK * D, bytes_accessed=2 * TOK * D + 4 * HALF * QBLK, transcendentals=FW * TOK),
    )(core, order, gate_up_t, out_grad, codes, scales)


def grads_kernel(place_ref, gate_up_ref, own_hbm, core_hbm, x_hbm, both_hbm, out_grad_hbm, out_ref, weight, out_grad, weight_sems, sems):
    reads = []
    for i, part in enumerate((own_hbm, core_hbm, x_hbm, both_hbm)):
        row = pl.multiple_of(jnp.bitwise_xor(place_ref[0], i) * PAD_ROWS, PAD_ROWS)
        reads.append(pltpu.make_async_copy(part, weight.at[pl.ds(row, PAD_ROWS), :], weight_sems.at[i]))
        reads[-1].start()
    for chunk in range(GRAD_STEPS):
        read_columns(out_grad_hbm, out_grad, sems, chunk, GRAD_WIDTH).start()
    both = gate_up_ref[...].astype(jnp.float32)
    gate, up = both[:FW], both[FW:]
    sig = jax.nn.sigmoid(gate)
    for read in reads:
        read.wait()
    total = jnp.zeros((TOK, 4 * PAD_ROWS), jnp.float32)
    for chunk in range(GRAD_STEPS):
        columns = slice(chunk * GRAD_WIDTH, (chunk + 1) * GRAD_WIDTH)
        read_columns(out_grad_hbm, out_grad, sems, chunk, GRAD_WIDTH).wait()
        total += lax.dot_general(
            out_grad[:, columns], weight[:, columns], (((1,), (1,)), ((), ())), preferred_element_type=jnp.float32
        )
    total = total.T
    hidden_grad = jnp.concatenate([total[i * PAD_ROWS : i * PAD_ROWS + NODE_ROWS, :] for i in range(4)], axis=0)
    gate_grad = hidden_grad * up * sig * (1.0 + gate * (1.0 - sig))
    up_grad = hidden_grad * (gate * sig)
    out_ref[...] = jnp.concatenate([gate_grad, up_grad], axis=0).astype(jnp.bfloat16)


def input_grads(place, gate_up_t, parts, out_grad):
    smem = pl.BlockSpec(memory_space=pltpu.SMEM)
    vmem = pl.BlockSpec(memory_space=pltpu.VMEM)
    anywhere = pl.BlockSpec(memory_space=pl.ANY)
    return pl.pallas_call(
        grads_kernel,
        in_specs=[smem, vmem] + [anywhere] * 4 + [pl.BlockSpec(memory_space=pltpu.HBM)],
        out_specs=vmem,
        scratch_shapes=[
            pltpu.VMEM((4 * PAD_ROWS, D), jnp.bfloat16),
            pltpu.VMEM((TOK, D), jnp.bfloat16),
            pltpu.SemaphoreType.DMA((4,)),
            pltpu.SemaphoreType.DMA((GRAD_STEPS,)),
        ],
        out_shape=jax.ShapeDtypeStruct((2 * FW, TOK), jnp.bfloat16),
        compiler_params=pltpu.CompilerParams(vmem_limit_bytes=56 * 2**20),
        cost_estimate=pl.CostEstimate(flops=2 * FW * TOK * D, bytes_accessed=2 * TOK * D + 2 * 128 * D, transcendentals=FW * TOK),
    )(place, gate_up_t, *parts, out_grad)


def last_sum_kernel(got_ref, out_ref, total):
    rows = 8 * SPAN
    eight = got_ref[:rows, :].astype(jnp.float32)
    for i in range(1, XROWS // rows):
        eight += got_ref[i * rows : (i + 1) * rows, :].astype(jnp.float32)
    total[...] = eight
    span = total[:SPAN, :]
    for i in range(1, 8):
        span += total[i * SPAN : (i + 1) * SPAN, :]
    span = span * (1.0 / DEVICES)
    for i in range(SPAN):
        out_ref[:, i * QBLK : (i + 1) * QBLK] = span[i : i + 1, :]


def last_sum(got):
    return pl.pallas_call(
        last_sum_kernel,
        in_specs=[pl.BlockSpec(memory_space=pltpu.VMEM)],
        out_specs=pl.BlockSpec(memory_space=pltpu.VMEM),
        out_shape=jax.ShapeDtypeStruct((1, SPAN * QBLK), jnp.float32),
        scratch_shapes=[pltpu.VMEM((8 * SPAN, QBLK), jnp.float32)],
        compiler_params=pltpu.CompilerParams(vmem_limit_bytes=2 * 2**20),
    )(got)


def per_device(gate_up, out_grad, weight_codes, weight_scales, shard_order):
    gate_up_t = gate_up.T
    core = lax.axis_index("core").astype(jnp.int32).reshape(1)
    place = lax.axis_index(("xl", "core")).astype(jnp.int32).reshape(1)
    keep, send, weight = partial_spans(shard_order, core, gate_up_t, out_grad, weight_codes, weight_scales)
    got = lax.ppermute(send, "core", SWAP)
    pair = (keep.astype(jnp.float32) + got.astype(jnp.float32)).astype(jnp.bfloat16)
    got = lax.all_to_all(pair, ("xh", "xl"), split_axis=0, concat_axis=0, tiled=True)
    parts = [got[i * XROWS : (i + 1) * XROWS].astype(jnp.float32) for i in range(NX)]
    line = (parts[0] + parts[1] + parts[2] + parts[3]).astype(jnp.bfloat16)
    weight, line = lax.optimization_barrier((weight, line))
    weight_x = lax.ppermute(weight, XC, OPPOSITE)
    weight_core = lax.ppermute(weight, "core", SWAP)
    weight_both = lax.ppermute(weight_x, "core", SWAP)
    got = lax.all_to_all(line.reshape(XROWS // 2, 2, QBLK), ("y", "z"), split_axis=0, concat_axis=0, tiled=True)
    grads = input_grads(place, gate_up_t, (weight, weight_core, weight_x, weight_both), out_grad)
    got, grads = lax.optimization_barrier((got, grads))
    weight_grad = last_sum(got.reshape(XROWS, QBLK))
    return (grads.T, weight_grad)


def solution(mesh):
    fine = Mesh(mesh.devices.reshape(NY, NZ, 2, 2, 2), ALL)
    return jax.shard_map(
        per_device,
        mesh=fine,
        in_specs=(P(ALL, None), P(ALL, None), P(("xl", "core"), None), P(("xl", "core"), None), P()),
        out_specs=(P(ALL, None), P(ALL, None)),
        check_vma=False,
    )
```

```python
import jax
import jax.numpy as jnp
from jax import lax
from jax.experimental import pallas as pl
from jax.experimental.pallas import tpu as pltpu
from jax.sharding import Mesh
from jax.sharding import PartitionSpec as P

D = 8192
FW = 120
TOK = 256
QBLK = 128
SPAN = 10
DEVICES = 768
NY, NZ = 8, 12
NX = 4
ROWS = DEVICES * SPAN
HALF = ROWS // 2
NODE_ROWS = 30
PAD_ROWS = 32
BLOCKS = D // QBLK
STEP_BLOCKS = 16
STEPS = BLOCKS // STEP_BLOCKS
WIDTH = STEP_BLOCKS * QBLK
GRAD_STEPS = 2
GRAD_WIDTH = D // GRAD_STEPS
SWAP = [(0, 1), (1, 0)]
OPPOSITE = [(x * 2 + c, (x + (1 if (x + c) % 2 == 0 else -1)) % NX * 2 + c) for x in range(NX) for c in range(2)]
XROWS = HALF // NX
ALL = ("y", "z", "xh", "xl", "core")
XC = ("xh", "xl", "core")


def read_columns(source, target, sems, chunk, width=WIDTH):
    columns = pl.ds(chunk * width, width)
    return pltpu.make_async_copy(source.at[:, columns], target.at[:, columns], sems.at[chunk])


def partial_kernel(
    core_ref, order_hbm, gate_up_hbm, out_grad_hbm, codes_hbm, scales_hbm, keep_hbm, send_hbm, weight_hbm,
    order, gate_up, codes, scales, out_grad, blocks, staged, spans_out, weight_out, sems, small_sems, write_sems,
):
    small = [
        pltpu.make_async_copy(source, target, small_sems.at[i])
        for i, (source, target) in enumerate(
            ((gate_up_hbm, gate_up), (scales_hbm, scales), (codes_hbm, codes), (order_hbm, order))
        )
    ]
    small[0].start()
    for chunk in range(STEPS):
        read_columns(out_grad_hbm, out_grad, sems, chunk).start()
    for read in small[1:]:
        read.start()
    small[0].wait()
    both = gate_up[...].astype(jnp.float32)
    gate, up = both[:FW], both[FW:]
    hidden = (gate * jax.nn.sigmoid(gate) * up).astype(jnp.bfloat16)
    for chunk in range(STEPS):
        columns = slice(chunk * WIDTH, (chunk + 1) * WIDTH)
        read_columns(out_grad_hbm, out_grad, sems, chunk).wait()
        product = jnp.dot(hidden, out_grad[:, columns], preferred_element_type=jnp.float32)
        for block in range(STEP_BLOCKS):
            blocks[pl.ds(chunk * STEP_BLOCKS + block, FW, stride=BLOCKS), :] = product[:, block * QBLK : (block + 1) * QBLK]
    for read in small[1:]:
        read.wait()
    fill = jnp.zeros((PAD_ROWS - NODE_ROWS, WIDTH), jnp.float32)
    for chunk in range(STEPS):
        columns = slice(chunk * WIDTH, (chunk + 1) * WIDTH)
        block_of = lax.broadcasted_iota(jnp.int32, (BLOCKS, WIDTH), 1) // QBLK + chunk * STEP_BLOCKS
        one_hot = (lax.broadcasted_iota(jnp.int32, (BLOCKS, WIDTH), 0) == block_of).astype(jnp.float32)
        wide = jnp.dot(scales[...], one_hot.astype(jnp.bfloat16), preferred_element_type=jnp.float32)
        weight = codes[:, columns].astype(jnp.float32) * wide
        weight_out[:, columns] = jnp.concatenate([weight, fill], axis=0).astype(jnp.bfloat16)

    weight_write = pltpu.make_async_copy(weight_out, weight_hbm, write_sems.at[2 * NX])
    weight_write.start()
    core = core_ref[0]
    writes = [weight_write]
    for side, (owner_core, target) in enumerate(((core, keep_hbm), (1 - core, send_hbm))):
        for x in range(NX):
            rows = pl.ds(x * XROWS, XROWS)

            def gather(zy, carry):
                owner = ((zy & (NY - 1)) * NZ + (zy >> 3)) * 8 + x * 2 + owner_core
                span = order[owner]
                staged[pl.ds(zy * SPAN, SPAN), :] = blocks[pl.ds(span * SPAN, SPAN), :]
                return carry

            lax.fori_loop(0, NY * NZ, gather, 0, unroll=32)
            spans_out[side, rows, :] = staged[...].astype(jnp.bfloat16)
            write = pltpu.make_async_copy(spans_out.at[side, rows, :], target.at[rows, :], write_sems.at[side * NX + x])
            write.start()
            writes.append(write)
    for write in writes:
        write.wait()


def partial_spans(order, core, gate_up_t, out_grad, codes, scales):
    hbm = pl.BlockSpec(memory_space=pltpu.HBM)
    return pl.pallas_call(
        partial_kernel,
        in_specs=[pl.BlockSpec(memory_space=pltpu.SMEM)] + [hbm] * 5,
        out_specs=[hbm, hbm, hbm],
        scratch_shapes=[
            pltpu.SMEM((DEVICES,), jnp.int32),
            pltpu.VMEM((2 * FW, TOK), jnp.bfloat16),
            pltpu.VMEM((NODE_ROWS, D), jnp.bfloat16),
            pltpu.VMEM((NODE_ROWS, BLOCKS), jnp.bfloat16),
            pltpu.VMEM((TOK, D), jnp.bfloat16),
            pltpu.VMEM((ROWS, QBLK), jnp.float32),
            pltpu.VMEM((XROWS, QBLK), jnp.float32),
            pltpu.VMEM((2, HALF, QBLK), jnp.bfloat16),
            pltpu.VMEM((PAD_ROWS, D), jnp.bfloat16),
            pltpu.SemaphoreType.DMA((STEPS,)),
            pltpu.SemaphoreType.DMA((4,)),
            pltpu.SemaphoreType.DMA((2 * NX + 1,)),
        ],
        out_shape=[
            jax.ShapeDtypeStruct((HALF, QBLK), jnp.bfloat16),
            jax.ShapeDtypeStruct((HALF, QBLK), jnp.bfloat16),
            jax.ShapeDtypeStruct((PAD_ROWS, D), jnp.bfloat16),
        ],
        compiler_params=pltpu.CompilerParams(vmem_limit_bytes=56 * 2**20),
        cost_estimate=pl.CostEstimate(flops=2 * FW * TOK * D, bytes_accessed=2 * TOK * D + 4 * HALF * QBLK, transcendentals=FW * TOK),
    )(core, order, gate_up_t, out_grad, codes, scales)


def grads_kernel(place_ref, gate_up_ref, own_hbm, core_hbm, x_hbm, both_hbm, out_grad_hbm, out_ref, weight, out_grad, weight_sems, sems):
    reads = []
    for i, part in enumerate((own_hbm, core_hbm, x_hbm, both_hbm)):
        row = pl.multiple_of(jnp.bitwise_xor(place_ref[0], i) * PAD_ROWS, PAD_ROWS)
        reads.append(pltpu.make_async_copy(part, weight.at[pl.ds(row, PAD_ROWS), :], weight_sems.at[i]))
        reads[-1].start()
    for chunk in range(GRAD_STEPS):
        read_columns(out_grad_hbm, out_grad, sems, chunk, GRAD_WIDTH).start()
    both = gate_up_ref[...].astype(jnp.float32)
    gate, up = both[:FW], both[FW:]
    sig = jax.nn.sigmoid(gate)
    for read in reads:
        read.wait()
    total = jnp.zeros((TOK, 4 * PAD_ROWS), jnp.float32)
    for chunk in range(GRAD_STEPS):
        columns = slice(chunk * GRAD_WIDTH, (chunk + 1) * GRAD_WIDTH)
        read_columns(out_grad_hbm, out_grad, sems, chunk, GRAD_WIDTH).wait()
        total += lax.dot_general(
            out_grad[:, columns], weight[:, columns], (((1,), (1,)), ((), ())), preferred_element_type=jnp.float32
        )
    total = total.T
    hidden_grad = jnp.concatenate([total[i * PAD_ROWS : i * PAD_ROWS + NODE_ROWS, :] for i in range(4)], axis=0)
    gate_grad = hidden_grad * up * sig * (1.0 + gate * (1.0 - sig))
    up_grad = hidden_grad * (gate * sig)
    out_ref[...] = jnp.concatenate([gate_grad, up_grad], axis=0).astype(jnp.bfloat16)


def input_grads(place, gate_up_t, parts, out_grad):
    smem = pl.BlockSpec(memory_space=pltpu.SMEM)
    vmem = pl.BlockSpec(memory_space=pltpu.VMEM)
    anywhere = pl.BlockSpec(memory_space=pl.ANY)
    return pl.pallas_call(
        grads_kernel,
        in_specs=[smem, vmem] + [anywhere] * 4 + [pl.BlockSpec(memory_space=pltpu.HBM)],
        out_specs=vmem,
        scratch_shapes=[
            pltpu.VMEM((4 * PAD_ROWS, D), jnp.bfloat16),
            pltpu.VMEM((TOK, D), jnp.bfloat16),
            pltpu.SemaphoreType.DMA((4,)),
            pltpu.SemaphoreType.DMA((GRAD_STEPS,)),
        ],
        out_shape=jax.ShapeDtypeStruct((2 * FW, TOK), jnp.bfloat16),
        compiler_params=pltpu.CompilerParams(vmem_limit_bytes=56 * 2**20),
        cost_estimate=pl.CostEstimate(flops=2 * FW * TOK * D, bytes_accessed=2 * TOK * D + 2 * 128 * D, transcendentals=FW * TOK),
    )(place, gate_up_t, *parts, out_grad)


def last_sum_kernel(got_ref, out_ref, total):
    rows = 8 * SPAN
    eight = got_ref[:rows, :].astype(jnp.float32)
    for i in range(1, XROWS // rows):
        eight += got_ref[i * rows : (i + 1) * rows, :].astype(jnp.float32)
    total[...] = eight
    span = total[:SPAN, :]
    for i in range(1, 8):
        span += total[i * SPAN : (i + 1) * SPAN, :]
    span = span * (1.0 / DEVICES)
    for i in range(SPAN):
        out_ref[:, i * QBLK : (i + 1) * QBLK] = span[i : i + 1, :]


def last_sum(got):
    return pl.pallas_call(
        last_sum_kernel,
        in_specs=[pl.BlockSpec(memory_space=pltpu.VMEM)],
        out_specs=pl.BlockSpec(memory_space=pltpu.VMEM),
        out_shape=jax.ShapeDtypeStruct((1, SPAN * QBLK), jnp.float32),
        scratch_shapes=[pltpu.VMEM((8 * SPAN, QBLK), jnp.float32)],
        compiler_params=pltpu.CompilerParams(vmem_limit_bytes=2 * 2**20),
    )(got)


def per_device(gate_up, out_grad, weight_codes, weight_scales, shard_order):
    gate_up_t = gate_up.T
    core = lax.axis_index("core").astype(jnp.int32).reshape(1)
    place = lax.axis_index(("xl", "core")).astype(jnp.int32).reshape(1)
    keep, send, weight = partial_spans(shard_order, core, gate_up_t, out_grad, weight_codes, weight_scales)
    got = lax.ppermute(send, "core", SWAP)
    pair = (keep.astype(jnp.float32) + got.astype(jnp.float32)).astype(jnp.bfloat16)
    got = lax.all_to_all(pair, ("xh", "xl"), split_axis=0, concat_axis=0, tiled=True)
    parts = [got[i * XROWS : (i + 1) * XROWS].astype(jnp.float32) for i in range(NX)]
    line = (parts[0] + parts[1] + parts[2] + parts[3]).astype(jnp.bfloat16)
    weight, line = lax.optimization_barrier((weight, line))
    weight_x = lax.ppermute(weight, XC, OPPOSITE)
    weight_core = lax.ppermute(weight, "core", SWAP)
    weight_both = lax.ppermute(weight_x, "core", SWAP)
    got = lax.all_to_all(line.reshape(XROWS // 2, 2, QBLK), ("z", "y"), split_axis=0, concat_axis=0, tiled=True)
    grads = input_grads(place, gate_up_t, (weight, weight_core, weight_x, weight_both), out_grad)
    got, grads = lax.optimization_barrier((got, grads))
    weight_grad = last_sum(got.reshape(XROWS, QBLK))
    return (grads.T, weight_grad)


def solution(mesh):
    fine = Mesh(mesh.devices.reshape(NY, NZ, 2, 2, 2), ALL)
    return jax.shard_map(
        per_device,
        mesh=fine,
        in_specs=(P(ALL, None), P(ALL, None), P(("xl", "core"), None), P(("xl", "core"), None), P()),
        out_specs=(P(ALL, None), P(ALL, None)),
        check_vma=False,
    )
```
